256 devices in a mesh: gz: 4 (over x), gx: 16 (over z, core), gy: 4 (over y).
Axes of the slice: x: 4, y: 4, z: 8, core: 2. Of those that a mesh axis runs over, the one named last changes fastest.
Arguments:
- initial_heat_state: float32 [32, 512, 1024], P('gz', 'gx', 'gy'), may hold values from -6 to 6
- flow_speed_components: bfloat16 [3, 32, 512, 1024], P(None, 'gz', 'gx', 'gy'), may hold values from -4 to 4
- heat_spread_rate: float32 [32, 512, 1024], P('gz', 'gx', 'gy'), may hold values from 0.001 to 4
Outputs:
- advanced: float32 [32, 512, 1024], P('gz', 'gx', 'gy')
The draws below stay inside these ranges and needn't reach their ends.
All inputs are finite; a program needn't handle non-finite values.
Results may differ from the reference program's by a relative error of at most 0.0003.
Values sent between devices are 32-bit elements; how exact they have to be, the bound alone decides.
No kernel may reach another device: no remote copies, remote signals or barrier semaphores. Data moves between devices by JAX's collectives and lax.ppermute only.
A program may use at most 192 MiB of HBM per device.

```python
import math
import jax
import jax.numpy as jnp
from jax import lax

NZ = 32
NX = 512
NY = 1024


def draw_initial_heat_state(key, part):
    key = jax.random.fold_in(key, 3)
    random_subkeys = jax.random.split(key, 8)
    across_x = ((jnp.arange(NX, dtype=jnp.float32) + 0.5) / NX).reshape(1, NX, 1)
    along_y = ((jnp.arange(NY, dtype=jnp.float32) + 0.5) / NY).reshape(1, 1, NY)
    first_amount = 0.8 * jax.random.normal(random_subkeys[0], (NZ, 1, 1), jnp.float32)
    second_amount = 0.5 * jax.random.normal(random_subkeys[1], (NZ, 1, 1), jnp.float32)
    wave_x = 1.0 + 2.0 * jax.random.uniform(random_subkeys[2], (NZ, 1, 1), jnp.float32)
    wave_y = 1.0 + 2.0 * jax.random.uniform(random_subkeys[3], (NZ, 1, 1), jnp.float32)
    phase_along_x = jax.random.uniform(random_subkeys[4], (NZ, 1, 1), jnp.float32, 0.0, 2.0 * math.pi)
    phase_y = jax.random.uniform(random_subkeys[5], (NZ, 1, 1), jnp.float32, 0.0, 2.0 * math.pi)
    phase_both = jax.random.uniform(random_subkeys[6], (NZ, 1, 1), jnp.float32, 0.0, 2.0 * math.pi)
    smooth = first_amount * jnp.sin(math.pi * wave_x * across_x + phase_along_x) * jnp.sin(math.pi * wave_y * along_y + phase_y)
    smooth = smooth + second_amount * jnp.cos(2.0 * math.pi * (across_x + along_y) + phase_both)
    rough_part = jnp.clip(jax.random.normal(random_subkeys[7], (NZ, NX, NY), jnp.float32), -4.0, 4.0)
    return jnp.clip(smooth + rough_part, -6.0, 6.0).astype(jnp.float32)


def draw_heat_spread_rate(key, part):
    key = jax.random.fold_in(key, 7)
    random_subkeys = jax.random.split(key, 4)
    across_x = ((jnp.arange(NX, dtype=jnp.float32) + 0.5) / NX).reshape(1, NX, 1)
    along_y = ((jnp.arange(NY, dtype=jnp.float32) + 0.5) / NY).reshape(1, 1, NY)
    phase_x = jax.random.uniform(random_subkeys[0], (), jnp.float32, 0.0, 2.0 * math.pi)
    phase_y = jax.random.uniform(random_subkeys[1], (), jnp.float32, 0.0, 2.0 * math.pi)
    ridge = jnp.sin(2.0 * math.pi * across_x + phase_x) + jnp.sin(2.0 * math.pi * along_y + phase_y)
    weight = jax.nn.sigmoid(10.0 * (ridge - 1.0))
    main_rate = jnp.exp(jax.random.uniform(random_subkeys[2], (NZ, NX, NY), jnp.float32, math.log(0.25), math.log(4.0)))
    quiet_rate = jnp.exp(jax.random.uniform(random_subkeys[3], (NZ, NX, NY), jnp.float32, math.log(0.001), math.log(0.004)))
    log_rate = (1.0 - weight) * jnp.log(main_rate) + weight * jnp.log(quiet_rate)
    return jnp.clip(jnp.exp(log_rate), 0.001, 4.0).astype(jnp.float32)


def block_levels(stream_key, extent, cuts, least, largest):
    gain = 1.0
    for axis_at, blocks in cuts:
        heights = jax.random.uniform(jax.random.fold_in(jax.random.fold_in(stream_key, 6), axis_at), (blocks,), jnp.float32, least / len(cuts), largest / len(cuts))
        gain = gain * jnp.repeat(jnp.exp(heights), extent[axis_at] // blocks).reshape((-1,) + (1,) * (len(extent) - 1 - axis_at))
    return gain


def gaussian(key, dims, scale, bound, shards=(), kind=jnp.bfloat16):
    drawn = scale * jax.random.normal(key, dims, jnp.float32)
    if shards:
        drawn = drawn * block_levels(key, dims, shards, -0.22, 0.18)
    return jnp.clip(drawn, -bound, bound).astype(kind)


def setup_inputs(seed: int = 0) -> dict:
    seeds = jax.random.split(jax.random.key(seed), 4)
    return {
        "initial_heat_state": draw_initial_heat_state(jax.random.fold_in(seeds[3], 71), 0),
        "flow_speed_components": gaussian(seeds[1], (3, NZ, NX, NY), 1.0, 4.0, ((1, 4), (2, 16), (3, 4))),
        "heat_spread_rate": draw_heat_spread_rate(jax.random.fold_in(seeds[3], 71), 0),
    }


advect_number = 0.5
vertical_number = 0.06

def neighbour_coefficients(scalar_field, flow_speed_components, heat_spread_rate):
    padded = jnp.pad(scalar_field, 1)
    above = padded[2:, 1:-1, 1:-1]
    below = padded[:-2, 1:-1, 1:-1]
    east = padded[1:-1, 2:, 1:-1]
    west = padded[1:-1, :-2, 1:-1]
    north = padded[1:-1, 1:-1, 2:]
    south = padded[1:-1, 1:-1, :-2]
    wind = flow_speed_components.astype(jnp.float32)
    transport = wind[0] * (above - below) + wind[1] * (east - west) + wind[2] * (north - south)
    return scalar_field - 0.5 * advect_number * transport + vertical_number * heat_spread_rate * (above + below - 2.0 * scalar_field)

def implicit_lines(right_side, heat_spread_rate, line_axis):
    reach_square = NX / 8.0 * (NX / 8.0)
    moved = jnp.moveaxis(right_side, line_axis, -1)
    moved_kappa = jnp.moveaxis(heat_spread_rate, line_axis, -1)
    coupling = -reach_square * moved_kappa
    count = moved.shape[-1]
    position = lax.broadcasted_iota(jnp.int32, moved.shape, moved.ndim - 1)
    sub_band = jnp.where(position == 0, jnp.zeros_like(coupling), coupling)
    super_band = jnp.where(position == count - 1, jnp.zeros_like(coupling), coupling)
    centre = 1.0 + 2.0 * reach_square * moved_kappa
    solved = lax.linalg.tridiagonal_solve(sub_band, centre, super_band, moved[..., None])[..., 0]
    return jnp.moveaxis(solved, -1, line_axis)

def reference(initial_heat_state, flow_speed_components, heat_spread_rate):
    forward_known_term = neighbour_coefficients(initial_heat_state, flow_speed_components, heat_spread_rate)
    swept_x = implicit_lines(forward_known_term, heat_spread_rate, 1)
    swept_y = implicit_lines(swept_x, heat_spread_rate, 2)
    return neighbour_coefficients(swept_y, flow_speed_components, heat_spread_rate)
```

```python
import functools
import jax
import jax.numpy as jnp
from jax import lax
from jax.experimental import pallas as pl
from jax.experimental.pallas import tpu as pltpu
from jax.sharding import PartitionSpec as P


QUARTER = 0.25
VERTICAL = 0.06
VMEM_BYTES = 24 * 2**20


def call(kernel, outs, *ins, name, flops=0):
    shapes = [jax.ShapeDtypeStruct(s, jnp.float32) for s in outs]
    vm = pl.BlockSpec(memory_space=pltpu.VMEM)
    size = 4 * (sum(x.size for x in ins) + sum(x.size for x in shapes))
    return pl.pallas_call(
        kernel,
        out_shape=shapes,
        in_specs=[vm] * len(ins),
        out_specs=[vm] * len(outs),
        compiler_params=pltpu.CompilerParams(vmem_limit_bytes=VMEM_BYTES),
        cost_estimate=pl.CostEstimate(flops=flops, bytes_accessed=size, transcendentals=0),
        name=name,
    )(*ins)


def merge(a, b):
    a0, a1, aL, aC, aR = a
    b0, b1, bL, bC, bR = b
    inv = 1.0 / (1.0 - aR * bL)
    x = aC * inv
    y = bC * inv
    return (
        a0 + x * (b0 + bL * a1),
        b1 + y * (a1 + aR * b0),
        aL + x * bL * aC,
        x * bC,
        bR + y * aR * bC,
    )


def close_left(p, g, block):
    b0, b1, bL, bC, bR = block
    f = bC / (1.0 - bL * g)
    return b1 + bC * p + f * g * (b0 + bL * p), bR + f * g * bC


def close_right(p, g, block):
    b0, b1, bL, bC, bR = block
    f = bC / (1.0 - bR * g)
    return b0 + bC * p + f * g * (b1 + bR * p), bL + f * g * bC


def chain_ends(blocks, index):
    zero = jnp.zeros_like(blocks[0][0])
    p, g = zero, zero
    lp, lg = zero, zero
    for m in range(len(blocks) - 1):
        p, g = close_left(p, g, blocks[m])
        here = index == m + 1
        lp, lg = jnp.where(here, p, lp), jnp.where(here, g, lg)
    p, g = zero, zero
    rp, rg = zero, zero
    for m in range(len(blocks) - 1, 0, -1):
        p, g = close_right(p, g, blocks[m])
        here = index == m - 1
        rp, rg = jnp.where(here, p, rp), jnp.where(here, g, rg)
    return lp, lg, rp, rg


def factor(d_ref, w_ref, l_ref, r_ref, count):
    delta = 1.0 + d_ref[0]
    w = 1.0 / (1.0 + delta)
    w_ref[0] = w
    y = jnp.ones_like(w)
    l_ref[0] = y
    for i in range(1, count):
        y = y * w
        l_ref[i] = y
        delta = d_ref[i] + delta * w
        w = 1.0 / (1.0 + delta)
        w_ref[i] = w
    r = w
    s = w * y
    r_ref[count - 1] = r
    l_ref[count - 1] = s
    for i in range(count - 2, -1, -1):
        w = w_ref[i]
        r = w * r
        s = w * (l_ref[i] + s)
        r_ref[i] = r
        l_ref[i] = s


def sweep(q, w_ref, out_ref, count):
    y = q(0)
    out_ref[0] = y
    for i in range(1, count):
        y = q(i) + w_ref[i - 1] * y
        out_ref[i] = y
    s = w_ref[count - 1] * y
    out_ref[count - 1] = s
    for i in range(count - 2, -1, -1):
        s = w_ref[i] * (out_ref[i] + s)
        out_ref[i] = s


def pack(v, half, h):
    piece = v[h * half : (h + 1) * half]
    mid = v.shape[1] // 2
    return jnp.concatenate([piece[:, :mid], piece[:, mid:]], axis=0)


def unpack(v):
    half = v.shape[0] // 2
    return jnp.concatenate([v[:half], v[half:]], axis=1)


def stencil(z, f, below, above, west, east, ydiff, wind_ref, k):
    count = f.shape[0]
    row = lax.broadcasted_iota(jnp.int32, f.shape, 0)
    e = jnp.where(row == count - 1, east, pltpu.roll(f, count - 1, 0))
    w = jnp.where(row == 0, west, pltpu.roll(f, 1, 0))
    wz = wind_ref[0, z].astype(jnp.float32)
    wx = wind_ref[1, z].astype(jnp.float32)
    wy = wind_ref[2, z].astype(jnp.float32)
    return (
        f
        - QUARTER * (wz * (above - below) + wx * (e - w) + wy * ydiff)
        + VERTICAL * k * (above + below - 2.0 * f)
    )


def body(field, wind, rate):
    nz, nx, ny = field.shape
    lines = nz * nx
    members = lax.axis_size("gx")
    chips = members // 2
    levels = lax.axis_size("gz")
    columns = lax.axis_size("gy")
    reach = nx * members / 8.0
    c = reach * reach
    subs = 8
    steps = ny // subs
    half = nz // 2
    face = (2 * half, ny // 2)

    def core():
        return lax.rem(lax.axis_index("gx"), 2)

    def faces_kernel(f_ref, zlo, zhi, ylo, yhi, xc, xi):
        zlo[...] = f_ref[0]
        zhi[...] = f_ref[nz - 1]
        flat = f_ref[...].reshape(lines, ny)
        ylo[...] = flat[:, :128].T[:8]
        yhi[...] = flat[:, ny - 128 :].T[120:]
        first, last = f_ref[:, 0, :], f_ref[:, nx - 1, :]
        odd = core() == 1
        xc[...] = jnp.where(odd, last, first)
        xi[...] = jnp.where(odd, first, last)

    def up(a, axis):
        n = lax.axis_size(axis)
        return lax.ppermute(a, axis, [(i, (i + 1) % n) for i in range(n)])

    def down(a, axis):
        n = lax.axis_size(axis)
        return lax.ppermute(a, axis, [((i + 1) % n, i) for i in range(n)])

    def across(a):
        return lax.ppermute(a, "gx", [(i, (i + 1 if i % 2 else i - 1) % members) for i in range(members)])

    def sibling(a):
        return lax.ppermute(a, "gx", [(i, i ^ 1) for i in range(members)])

    def x_rows(cross, inner):
        index = lax.axis_index("gx")
        odd = core() == 1
        west = jnp.where(index == 0, 0.0, jnp.where(odd, inner, cross))
        east = jnp.where(index == members - 1, 0.0, jnp.where(odd, cross, inner))
        return west, east

    def z_planes(below, above):
        index = lax.axis_index("gz")
        return jnp.where(index == 0, 0.0, below), jnp.where(index == levels - 1, 0.0, above)

    def x_matrix_kernel(k_ref, d_ref, w_ref, l_ref, r_ref):
        d_ref[...] = 1.0 / (c * jnp.swapaxes(k_ref[...], 0, 1))
        factor(d_ref, w_ref, l_ref, r_ref, nx)

    def y_matrix_kernel(dx_ref, d_ref, w_ref, l_ref, r_ref, c_ref):
        d_ref[...] = jnp.swapaxes(dx_ref[...].reshape(lines, ny).T.reshape(subs, steps, lines), 0, 1)
        factor(d_ref, w_ref, l_ref, r_ref, steps)
        L, C, R = l_ref[0], r_ref[0], r_ref[steps - 1]
        for level in range(3):
            shift = subs - (1 << level)
            bL, bC, bR = pltpu.roll(L, shift, 0), pltpu.roll(C, shift, 0), pltpu.roll(R, shift, 0)
            inv = 1.0 / (1.0 - R * bL)
            x, y = C * inv, bC * inv
            for n, value in enumerate((x, y, bL, R, bC, inv, R * y)):
                c_ref[level, n] = value
            L, C, R = L + x * bL * C, x * bC, bR + y * R * bC
        c_ref[3, 0], c_ref[3, 1], c_ref[3, 2] = L, C, R

    def explicit_kernel(
        f_ref, wind_ref, k_ref, below, above, south, north, xc, xi, d_ref, w_ref, l_ref, r_ref,
        base_ref, mine_ref, send_ref, e_ref,
    ):
        west, east = x_rows(xc[...], xi[...])
        low, high = z_planes(below[...], above[...])
        gy = lax.axis_index("gy")
        left = jnp.where(gy == 0, 0.0, south[7:8])
        right = jnp.where(gy == columns - 1, 0.0, north[0:1])
        left = jnp.broadcast_to(left, (128, lines)).T
        right = jnp.broadcast_to(right, (128, lines)).T
        lane = lax.broadcasted_iota(jnp.int32, (nx, 128), 1)
        for z in range(nz):
            f = f_ref[z]
            rows = slice(z * nx, (z + 1) * nx)
            no = pltpu.roll(f, ny - 1, 1)
            so = pltpu.roll(f, 1, 1)
            no = jnp.concatenate([no[:, : ny - 128], jnp.where(lane == 127, right[rows], no[:, ny - 128 :])], axis=1)
            so = jnp.concatenate([jnp.where(lane == 0, left[rows], so[:, :128]), so[:, 128:]], axis=1)
            e_ref[z] = stencil(
                z, f,
                f_ref[z - 1] if z else low,
                f_ref[z + 1] if z < nz - 1 else high,
                west[z : z + 1], east[z : z + 1], no - so, wind_ref, k_ref[z],
            )
        e = jnp.swapaxes(e_ref[...], 0, 1)
        sweep(lambda i: e[i] * d_ref[i], w_ref, base_ref, nx)
        odd = core() == 1
        ends = (base_ref[0], base_ref[nx - 1], l_ref[0], r_ref[0], r_ref[nx - 1])
        for n, v in enumerate(ends):
            lo, hi = pack(v, half, 0), pack(v, half, 1)
            mine_ref[n] = jnp.where(odd, hi, lo)
            send_ref[n] = jnp.where(odd, lo, hi)

    def pair(mine_ref, got_ref):
        odd = core() == 1
        a = tuple(jnp.where(odd, got_ref[n], mine_ref[n]) for n in range(5))
        b = tuple(jnp.where(odd, mine_ref[n], got_ref[n]) for n in range(5))
        return a, b

    def chip_kernel(mine_ref, got_ref, out_ref):
        whole = merge(*pair(mine_ref, got_ref))
        for n in range(5):
            for m in range(chips):
                out_ref[m, n] = whole[n]

    def x_chain_kernel(all_ref, mine_ref, got_ref, own_ref, send_ref):
        a, b = pair(mine_ref, got_ref)
        blocks = [tuple(all_ref[m, n] for n in range(5)) for m in range(chips)]
        lp, lg, rp, rg = chain_ends(blocks, lax.axis_index("gx") // 2)
        ap, ag = close_left(lp, lg, a)
        bp, bg = close_right(rp, rg, b)
        last_a = (ap + ag * bp) / (1.0 - ag * bg)
        first_b = bp + bg * last_a
        first_a = (a[0] + a[2] * lp + a[3] * first_b) / (1.0 - a[2] * lg)
        last_b = (b[1] + b[4] * rp + b[3] * last_a) / (1.0 - b[4] * rg)
        outer_l = lp + lg * first_a
        outer_r = rp + rg * last_b
        odd = core() == 1
        own_ref[0] = jnp.where(odd, last_a, outer_l)
        own_ref[1] = jnp.where(odd, outer_r, first_b)
        send_ref[0] = jnp.where(odd, outer_l, last_a)
        send_ref[1] = jnp.where(odd, first_b, outer_r)

    def x_finish_kernel(
        own_ref, got_ref, base_ref, l_ref, r_ref, d_ref, w_ref, c_ref,
        ybase_ref, up_ref, send_ref, s_ref,
    ):
        odd = core() == 1
        sides = []
        for n in range(2):
            own, got = unpack(own_ref[n]), unpack(got_ref[n])
            sides.append(jnp.concatenate([jnp.where(odd, got, own), jnp.where(odd, own, got)], axis=0))
        for i in range(nx):
            s_ref[i] = base_ref[i] + l_ref[i] * sides[0] + r_ref[i] * sides[1]
        t = s_ref[...].reshape(lines, ny).T
        q = jnp.swapaxes(t.reshape(subs, steps, lines), 0, 1)
        sweep(lambda i: q[i] * d_ref[i], w_ref, ybase_ref, steps)
        b0, b1 = ybase_ref[0], ybase_ref[steps - 1]
        for level in range(3):
            shift = subs - (1 << level)
            o0, o1 = pltpu.roll(b0, shift, 0), pltpu.roll(b1, shift, 0)
            x, y, bL, aR, _, inv, _ = (c_ref[level, n] for n in range(7))
            inner = b1 + aR * o0
            up_ref[level, 0] = inner * inv
            up_ref[level, 1] = o0
            b0, b1 = b0 + x * (o0 + bL * b1), o1 + y * inner
        for n, v in enumerate((b0, b1, c_ref[3, 0], c_ref[3, 1], c_ref[3, 2])):
            send_ref[n : n + 1] = v[0:1]
        send_ref[5:8] = jnp.zeros((3, lines), jnp.float32)

    def y_finish_kernel(
        own_ref, *refs,
    ):
        got, (ybase_ref, up_ref, l_ref, r_ref, c_ref), (s_ref, yd_ref, xc, xi, zlo, zhi) = (
            refs[: columns - 1], refs[columns - 1 : columns + 4], refs[columns + 4 :],
        )
        index = lax.axis_index("gy")
        messages = [own_ref[...]] + [ref[...] for ref in got]
        blocks = []
        for m in range(columns):
            v = messages[0]
            for back in range(1, columns):
                v = jnp.where(lax.rem(index - m + columns, columns) == back, messages[back], v)
            blocks.append(tuple(v[n : n + 1] for n in range(5)))
        mine = tuple(messages[0][n : n + 1] for n in range(5))
        lp, lg, rp, rg = chain_ends(blocks, index)
        p, g = close_left(lp, lg, mine)
        last = (p + g * rp) / (1.0 - g * rg)
        right = rp + rg * last
        first = (mine[0] + mine[2] * lp + mine[3] * right) / (1.0 - mine[2] * lg)
        left = lp + lg * first
        sub = lax.broadcasted_iota(jnp.int32, (subs, lines), 0)
        L = jnp.broadcast_to(left, (subs, lines))
        R = jnp.broadcast_to(right, (subs, lines))
        for level in (2, 1, 0):
            step = 1 << level
            x, _, bL, _, bC, _, z = (c_ref[level, n] for n in range(7))
            a = up_ref[level, 0] + x * L + z * R
            b = up_ref[level, 1] + bL * a + bC * R
            upper = (sub & step) != 0
            L, R = (
                jnp.where(upper, pltpu.roll(a, step, 0), L),
                jnp.where(upper, pltpu.roll(R, step, 0), b),
            )
        for i in range(steps):
            ybase_ref_i = ybase_ref[i] + l_ref[i] * L + r_ref[i] * R
            yd_ref[i] = ybase_ref_i
        s = jnp.swapaxes(yd_ref[...].reshape(steps, subs, lines), 0, 1).reshape(ny, lines)
        row = lax.broadcasted_iota(jnp.int32, s.shape, 0)
        north = jnp.where(row == ny - 1, right, pltpu.roll(s, ny - 1, 0))
        south = jnp.where(row == 0, left, pltpu.roll(s, 1, 0))
        yd_ref[...] = (north - south).reshape(yd_ref.shape)
        t = s.T
        odd = core() == 1
        low, high = t[:nz], t[lines - nz :]
        xc[...] = jnp.where(odd, high, low)
        xi[...] = jnp.where(odd, low, high)
        s_ref[...] = jnp.swapaxes(t.reshape(nx, nz, ny), 0, 1)
        zlo[...] = s_ref[0]
        zhi[...] = s_ref[nz - 1]

    def turn_kernel(yd_ref, out_ref):
        out_ref[...] = jnp.swapaxes(yd_ref[...].reshape(ny, lines).T.reshape(nx, nz, ny), 0, 1)

    def final_kernel(s_ref, yd_ref, wind_ref, k_ref, below, above, xc, xi, out_ref):
        west, east = x_rows(xc[...], xi[...])
        low, high = z_planes(below[...], above[...])
        for z in range(nz):
            out_ref[z] = stencil(
                z, s_ref[z],
                s_ref[z - 1] if z else low,
                s_ref[z + 1] if z < nz - 1 else high,
                west[z : z + 1], east[z : z + 1], yd_ref[z], wind_ref, k_ref[z],
            )

    box, xbox, ybox = (nz, nx, ny), (nx, nz, ny), (steps, subs, lines)
    five = (5,) + face

    zlo, zhi, ylo, yhi, xc, xi = call(
        faces_kernel, [(nx, ny), (nx, ny), (8, lines), (8, lines), (nz, ny), (nz, ny)], field, name="faces"
    )
    xc, xi = across(xc), sibling(xi)
    below, above = up(zhi, "gz"), down(zlo, "gz")
    south, north = up(yhi, "gy"), down(ylo, "gy")
    dx, wx, lx, rx = call(x_matrix_kernel, [xbox] * 4, rate, name="x_matrix", flops=10**6)
    dy, wy, ly, ry, cy = call(y_matrix_kernel, [ybox] * 4 + [(4, 7, subs, lines)], dx, name="y_matrix", flops=10**6)
    base, mine, send, _ = call(
        explicit_kernel, [xbox, five, five, box],
        field, wind, rate, below, above, south, north, xc, xi, dx, wx, lx, rx, name="explicit",
    )
    got = sibling(send)
    (spread,) = call(chip_kernel, [(chips,) + five], mine, got, name="chip")
    groups = [[2 * m + k for m in range(chips)] for k in range(2)]
    everyone = lax.all_to_all(spread, "gx", 0, 0, axis_index_groups=groups, tiled=True)
    own, send = call(x_chain_kernel, [(2,) + face] * 2, everyone, mine, got, name="x_chain")
    got = sibling(send)
    ybase, ups, send, _ = call(
        x_finish_kernel, [ybox, (3, 2, subs, lines), (8, lines), xbox],
        own, got, base, lx, rx, dy, wy, cy, name="x_finish",
    )
    ring = [
        lax.ppermute(send, "gy", [(i, (i + back) % columns) for i in range(columns)])
        for back in range(1, columns)
    ]
    swept, yd, xc, xi, zlo, zhi = call(
        y_finish_kernel, [box, ybox, (nz, ny), (nz, ny), (nx, ny), (nx, ny)],
        send, *ring, ybase, ups, ly, ry, cy, name="y_finish",
    )
    xc, xi = across(xc), sibling(xi)
    below, above = up(zhi, "gz"), down(zlo, "gz")
    (ydiff,) = call(turn_kernel, [box], yd, name="turn", flops=10**6)
    (out,) = call(final_kernel, [box], swept, ydiff, wind, rate, below, above, xc, xi, name="final")
    return out


def solution(mesh):
    in_specs = (P("gz", "gx", "gy"), P(None, "gz", "gx", "gy"), P("gz", "gx", "gy"))
    out_specs = P("gz", "gx", "gy")
    return jax.shard_map(body, mesh=mesh, in_specs=in_specs, out_specs=out_specs, check_vma=False)
```

```python
import functools
import jax
import jax.numpy as jnp
from jax import lax
from jax.experimental import pallas as pl
from jax.experimental.pallas import tpu as pltpu
from jax.sharding import PartitionSpec as P


QUARTER = 0.25
VERTICAL = 0.06
VMEM_BYTES = 24 * 2**20


def call(kernel, outs, *ins, name, flops=0, far=(), scratch=()):
    shapes = [jax.ShapeDtypeStruct(s, jnp.float32) if isinstance(s, tuple) else s for s in outs]
    vm = pl.BlockSpec(memory_space=pltpu.VMEM)
    any_space = pl.BlockSpec(memory_space=pltpu.HBM)
    size = 4 * (sum(x.size for x in ins) + sum(x.size for x in shapes))
    return pl.pallas_call(
        kernel,
        out_shape=shapes,
        in_specs=[any_space if n in far else vm for n in range(len(ins))],
        out_specs=[vm] * len(outs),
        scratch_shapes=list(scratch),
        compiler_params=pltpu.CompilerParams(vmem_limit_bytes=VMEM_BYTES),
        cost_estimate=pl.CostEstimate(flops=flops, bytes_accessed=size, transcendentals=0),
        name=name,
    )(*ins)


def merge(a, b):
    a0, a1, aL, aC, aR = a
    b0, b1, bL, bC, bR = b
    inv = 1.0 / (1.0 - aR * bL)
    x = aC * inv
    y = bC * inv
    return (
        a0 + x * (b0 + bL * a1),
        b1 + y * (a1 + aR * b0),
        aL + x * bL * aC,
        x * bC,
        bR + y * aR * bC,
    )


def close_left(p, g, block):
    b0, b1, bL, bC, bR = block
    f = bC / (1.0 - bL * g)
    return b1 + bC * p + f * g * (b0 + bL * p), bR + f * g * bC


def close_right(p, g, block):
    b0, b1, bL, bC, bR = block
    f = bC / (1.0 - bR * g)
    return b0 + bC * p + f * g * (b1 + bR * p), bL + f * g * bC


def chain_ends(blocks, index):
    zero = jnp.zeros_like(blocks[0][0])
    p, g = zero, zero
    lp, lg = zero, zero
    for m in range(len(blocks) - 1):
        p, g = close_left(p, g, blocks[m])
        here = index == m + 1
        lp, lg = jnp.where(here, p, lp), jnp.where(here, g, lg)
    p, g = zero, zero
    rp, rg = zero, zero
    for m in range(len(blocks) - 1, 0, -1):
        p, g = close_right(p, g, blocks[m])
        here = index == m - 1
        rp, rg = jnp.where(here, p, rp), jnp.where(here, g, rg)
    return lp, lg, rp, rg


def factor(d_ref, w_ref, l_ref, r_ref, count):
    delta = 1.0 + d_ref[0]
    w = 1.0 / (1.0 + delta)
    w_ref[0] = w
    y = jnp.ones_like(w)
    l_ref[0] = y
    for i in range(1, count):
        y = y * w
        l_ref[i] = y
        delta = d_ref[i] + delta * w
        w = 1.0 / (1.0 + delta)
        w_ref[i] = w
    r = w
    s = w * y
    r_ref[count - 1] = r
    l_ref[count - 1] = s
    for i in range(count - 2, -1, -1):
        w = w_ref[i]
        r = w * r
        s = w * (l_ref[i] + s)
        r_ref[i] = r
        l_ref[i] = s


def sweep(q, w_ref, out_ref, count):
    y = q(0)
    out_ref[0] = y
    for i in range(1, count):
        y = q(i) + w_ref[i - 1] * y
        out_ref[i] = y
    s = w_ref[count - 1] * y
    out_ref[count - 1] = s
    for i in range(count - 2, -1, -1):
        s = w_ref[i] * (out_ref[i] + s)
        out_ref[i] = s


def stencil(z, f, below, above, west, east, ydiff, wind_ref, k):
    count = f.shape[0]
    row = lax.broadcasted_iota(jnp.int32, f.shape, 0)
    e = jnp.where(row == count - 1, east, pltpu.roll(f, count - 1, 0))
    w = jnp.where(row == 0, west, pltpu.roll(f, 1, 0))
    wz = wind_ref[0, z].astype(jnp.float32)
    wx = wind_ref[1, z].astype(jnp.float32)
    wy = wind_ref[2, z].astype(jnp.float32)
    return (
        f
        - QUARTER * (wz * (above - below) + wx * (e - w) + wy * ydiff)
        + VERTICAL * k * (above + below - 2.0 * f)
    )


def body(field, wind, rate):
    nz, nx, ny = field.shape
    lines = nz * nx
    members = lax.axis_size("gx")
    chips = members // 2
    levels = lax.axis_size("gz")
    columns = lax.axis_size("gy")
    reach = nx * members / 8.0
    c = reach * reach
    subs = 8
    steps = ny // subs

    def core():
        return lax.rem(lax.axis_index("gx"), 2)

    def faces_kernel(f_ref, zlo, zhi, ylo, yhi, xc, xi):
        zlo[...] = f_ref[0]
        zhi[...] = f_ref[nz - 1]
        flat = f_ref[...].reshape(lines, ny)
        ylo[...] = flat[:, :128].T[:8]
        yhi[...] = flat[:, ny - 128 :].T[120:]
        first, last = f_ref[:, 0, :], f_ref[:, nx - 1, :]
        odd = core() == 1
        xc[...] = jnp.where(odd, last, first)
        xi[...] = jnp.where(odd, first, last)

    def up(a, axis):
        n = lax.axis_size(axis)
        return lax.ppermute(a, axis, [(i, (i + 1) % n) for i in range(n)])

    def down(a, axis):
        n = lax.axis_size(axis)
        return lax.ppermute(a, axis, [((i + 1) % n, i) for i in range(n)])

    def across(a):
        return lax.ppermute(a, "gx", [(i, (i + 1 if i % 2 else i - 1) % members) for i in range(members)])

    def sibling(a):
        return lax.ppermute(a, "gx", [(i, i ^ 1) for i in range(members)])

    def x_rows(cross, inner):
        index = lax.axis_index("gx")
        odd = core() == 1
        west = jnp.where(index == 0, 0.0, jnp.where(odd, inner, cross))
        east = jnp.where(index == members - 1, 0.0, jnp.where(odd, cross, inner))
        return west, east

    def z_planes(below, above):
        index = lax.axis_index("gz")
        return jnp.where(index == 0, 0.0, below), jnp.where(index == levels - 1, 0.0, above)

    def matrix_kernel(
        k_ref, far_wind, d_ref, w_ref, l_ref, r_ref, yd_ref, yw_ref, yl_ref, yr_ref, c_ref, wind_ref, sem
    ):
        fetch = pltpu.make_async_copy(far_wind, wind_ref, sem)
        fetch.start()
        d_ref[...] = 1.0 / (c * jnp.swapaxes(k_ref[...], 0, 1))
        factor(d_ref, w_ref, l_ref, r_ref, nx)
        yd_ref[...] = jnp.swapaxes(d_ref[...].reshape(lines, ny).T.reshape(subs, steps, lines), 0, 1)
        factor(yd_ref, yw_ref, yl_ref, yr_ref, steps)
        L, C, R = yl_ref[0], yr_ref[0], yr_ref[steps - 1]
        for level in range(3):
            shift = subs - (1 << level)
            bL, bC, bR = pltpu.roll(L, shift, 0), pltpu.roll(C, shift, 0), pltpu.roll(R, shift, 0)
            inv = 1.0 / (1.0 - R * bL)
            x, y = C * inv, bC * inv
            for n, value in enumerate((x, y, bL, R, bC, inv, R * y)):
                c_ref[level, n] = value
            L, C, R = L + x * bL * C, x * bC, bR + y * R * bC
        for n, value in enumerate((L, C, R)):
            c_ref[3, n] = value
        for n in range(3, 7):
            c_ref[3, n] = jnp.zeros_like(L)
        fetch.wait()

    def explicit_kernel(
        f_ref, wind_ref, k_ref, below, above, south, north, xc, xi, d_ref, w_ref, l_ref, r_ref,
        base_ref, ends_ref, e_ref,
    ):
        west, east = x_rows(xc[...], xi[...])
        low, high = z_planes(below[...], above[...])
        gy = lax.axis_index("gy")
        left = jnp.where(gy == 0, 0.0, south[7:8])
        right = jnp.where(gy == columns - 1, 0.0, north[0:1])
        left = jnp.broadcast_to(left, (128, lines)).T
        right = jnp.broadcast_to(right, (128, lines)).T
        lane = lax.broadcasted_iota(jnp.int32, (nx, 128), 1)
        for z in range(nz):
            f = f_ref[z]
            rows = slice(z * nx, (z + 1) * nx)
            no = pltpu.roll(f, ny - 1, 1)
            so = pltpu.roll(f, 1, 1)
            no = jnp.concatenate([no[:, : ny - 128], jnp.where(lane == 127, right[rows], no[:, ny - 128 :])], axis=1)
            so = jnp.concatenate([jnp.where(lane == 0, left[rows], so[:, :128]), so[:, 128:]], axis=1)
            e_ref[z] = stencil(
                z, f,
                f_ref[z - 1] if z else low,
                f_ref[z + 1] if z < nz - 1 else high,
                west[z : z + 1], east[z : z + 1], no - so, wind_ref, k_ref[z],
            )
        e = jnp.swapaxes(e_ref[...], 0, 1)
        sweep(lambda i: e[i] * d_ref[i], w_ref, base_ref, nx)
        ends = (base_ref[0], base_ref[nx - 1], l_ref[0], r_ref[0], r_ref[nx - 1])
        for n, v in enumerate(ends):
            ends_ref[n] = v

    def read(ref):
        return tuple(ref[n] for n in range(5))

    def choose(test, a, b):
        return tuple(jnp.where(test, x, y) for x, y in zip(a, b))

    def ordered(own_ref, got_ref, own_first):
        own, got = read(own_ref), read(got_ref)
        return choose(own_first, own, got), choose(own_first, got, own)

    def chip_kernel(own_ref, got_ref, out_ref):
        b0, b1, L, C, R = merge(*ordered(own_ref, got_ref, core() == 0))
        chip = lax.axis_index("gx") // 2
        first, last = chip == 0, chip == chips - 1
        L, R = jnp.where(first, 0.0, L), jnp.where(last, 0.0, R)
        C = jnp.where(jnp.logical_or(first, last), 0.0, C)
        for n, v in enumerate((b0, b1, L, C, R)):
            out_ref[n] = v

    def pair_kernel(own_ref, got_ref, out_ref):
        for n, v in enumerate(merge(*ordered(own_ref, got_ref, core() == 1))):
            out_ref[n] = v

    def side_kernel(near_ref, far_ref, opposite_ref, out_ref):
        three = merge(*ordered(near_ref, far_ref, core() == 1))
        four = merge(read(opposite_ref), three)
        for n, v in enumerate(choose(core() == 0, four, three)):
            out_ref[n] = v

    def x_finish_kernel(
        ends_ref, other_ref, side_ref, got_ref, base_ref, l_ref, r_ref, d_ref, w_ref, c_ref,
        ybase_ref, up_ref, send_ref, s_ref,
    ):
        odd = core() == 1
        chip = lax.axis_index("gx") // 2
        a, b = ordered(ends_ref, other_ref, core() == 0)
        left, right = ordered(side_ref, got_ref, core() == 0)
        zero = jnp.zeros_like(a[0])
        lp, lg = zero, zero
        for block in (right, left):
            lp, lg = close_left(lp, lg, block)
        rp, rg = zero, zero
        for block in (left, right):
            rp, rg = close_right(rp, rg, block)
        lp, lg = jnp.where(chip == 0, 0.0, lp), jnp.where(chip == 0, 0.0, lg)
        rp, rg = jnp.where(chip == chips - 1, 0.0, rp), jnp.where(chip == chips - 1, 0.0, rg)
        ap, ag = close_left(lp, lg, a)
        bp, bg = close_right(rp, rg, b)
        last_a = (ap + ag * bp) / (1.0 - ag * bg)
        first_b = bp + bg * last_a
        first_a = (a[0] + a[2] * lp + a[3] * first_b) / (1.0 - a[2] * lg)
        last_b = (b[1] + b[4] * rp + b[3] * last_a) / (1.0 - b[4] * rg)
        before = jnp.where(odd, last_a, lp + lg * first_a)
        after = jnp.where(odd, rp + rg * last_b, first_b)
        for i in range(nx):
            s_ref[i] = base_ref[i] + l_ref[i] * before + r_ref[i] * after
        t = s_ref[...].reshape(lines, ny).T
        q = jnp.swapaxes(t.reshape(subs, steps, lines), 0, 1)
        sweep(lambda i: q[i] * d_ref[i], w_ref, ybase_ref, steps)
        b0, b1 = ybase_ref[0], ybase_ref[steps - 1]
        for level in range(3):
            shift = subs - (1 << level)
            o0, o1 = pltpu.roll(b0, shift, 0), pltpu.roll(b1, shift, 0)
            x, y, bL, aR, _, inv, _ = (c_ref[level, n] for n in range(7))
            inner = b1 + aR * o0
            up_ref[level, 0] = inner * inv
            up_ref[level, 1] = o0
            b0, b1 = b0 + x * (o0 + bL * b1), o1 + y * inner
        for n, v in enumerate((b0, b1, c_ref[3, 0], c_ref[3, 1], c_ref[3, 2])):
            send_ref[n : n + 1] = v[0:1]
        send_ref[5:8] = jnp.zeros((3, lines), jnp.float32)

    def y_finish_kernel(
        own_ref, *refs,
    ):
        got, (ybase_ref, up_ref, l_ref, r_ref, c_ref), (s_ref, yd_ref, xc, xi, zlo, zhi) = (
            refs[: columns - 1], refs[columns - 1 : columns + 4], refs[columns + 4 :],
        )
        index = lax.axis_index("gy")
        messages = [own_ref[...]] + [ref[...] for ref in got]
        blocks = []
        for m in range(columns):
            v = messages[0]
            for back in range(1, columns):
                v = jnp.where(lax.rem(index - m + columns, columns) == back, messages[back], v)
            blocks.append(tuple(v[n : n + 1] for n in range(5)))
        mine = tuple(messages[0][n : n + 1] for n in range(5))
        lp, lg, rp, rg = chain_ends(blocks, index)
        p, g = close_left(lp, lg, mine)
        last = (p + g * rp) / (1.0 - g * rg)
        right = rp + rg * last
        first = (mine[0] + mine[2] * lp + mine[3] * right) / (1.0 - mine[2] * lg)
        left = lp + lg * first
        sub = lax.broadcasted_iota(jnp.int32, (subs, lines), 0)
        L = jnp.broadcast_to(left, (subs, lines))
        R = jnp.broadcast_to(right, (subs, lines))
        for level in (2, 1, 0):
            step = 1 << level
            x, _, bL, _, bC, _, z = (c_ref[level, n] for n in range(7))
            a = up_ref[level, 0] + x * L + z * R
            b = up_ref[level, 1] + bL * a + bC * R
            upper = (sub & step) != 0
            L, R = (
                jnp.where(upper, pltpu.roll(a, step, 0), L),
                jnp.where(upper, pltpu.roll(R, step, 0), b),
            )
        for i in range(steps):
            ybase_ref_i = ybase_ref[i] + l_ref[i] * L + r_ref[i] * R
            yd_ref[i] = ybase_ref_i
        s = jnp.swapaxes(yd_ref[...].reshape(steps, subs, lines), 0, 1).reshape(ny, lines)
        row = lax.broadcasted_iota(jnp.int32, s.shape, 0)
        north = jnp.where(row == ny - 1, right, pltpu.roll(s, ny - 1, 0))
        south = jnp.where(row == 0, left, pltpu.roll(s, 1, 0))
        yd_ref[...] = (north - south).reshape(yd_ref.shape)
        t = s.T
        odd = core() == 1
        low, high = t[:nz], t[lines - nz :]
        xc[...] = jnp.where(odd, high, low)
        xi[...] = jnp.where(odd, low, high)
        s_ref[...] = jnp.swapaxes(t.reshape(nx, nz, ny), 0, 1)
        zlo[...] = s_ref[0]
        zhi[...] = s_ref[nz - 1]

    def turn_kernel(yd_ref, out_ref):
        out_ref[...] = jnp.swapaxes(yd_ref[...].reshape(ny, lines).T.reshape(nx, nz, ny), 0, 1)

    def final_kernel(s_ref, yd_ref, wind_ref, k_ref, below, above, xc, xi, out_ref):
        west, east = x_rows(xc[...], xi[...])
        low, high = z_planes(below[...], above[...])
        for z in range(nz):
            out_ref[z] = stencil(
                z, s_ref[z],
                s_ref[z - 1] if z else low,
                s_ref[z + 1] if z < nz - 1 else high,
                west[z : z + 1], east[z : z + 1], yd_ref[z], wind_ref, k_ref[z],
            )

    box, xbox, ybox = (nz, nx, ny), (nx, nz, ny), (steps, subs, lines)
    five = (5, nz, ny)

    def outward(a, distance):
        move = lambda i: ((i // 2 + (-distance if i % 2 else distance)) % chips) * 2 + i % 2
        return lax.ppermute(a, "gx", [(i, move(i)) for i in range(members)])

    zlo, zhi, ylo, yhi, xc, xi = call(
        faces_kernel, [(nx, ny), (nx, ny), (8, lines), (8, lines), (nz, ny), (nz, ny)], field, name="faces"
    )
    xc, xi = across(xc), sibling(xi)
    below, above = up(zhi, "gz"), down(zlo, "gz")
    south, north = up(yhi, "gy"), down(ylo, "gy")
    dx, wx, lx, rx, dy, wy, ly, ry, cy, near_wind = call(
        matrix_kernel,
        [xbox] * 4 + [ybox] * 4 + [(4, 7, subs, lines), jax.ShapeDtypeStruct(wind.shape, wind.dtype)],
        rate, wind, name="matrix", flops=10**6, far=(1,), scratch=[pltpu.SemaphoreType.DMA],
    )
    base, ends, _ = call(
        explicit_kernel, [xbox, five, box],
        field, near_wind, rate, below, above, south, north, xc, xi, dx, wx, lx, rx, name="explicit",
    )
    other = sibling(ends)
    (chip,) = call(chip_kernel, [five], ends, other, name="chip")
    opposite = outward(chip, chips // 2)
    near = outward(chip, 1)
    (pair,) = call(pair_kernel, [five], chip, near, name="pair")
    distant = outward(pair, 2)
    (side,) = call(side_kernel, [five], near, distant, opposite, name="side")
    facing = sibling(side)
    ybase, ups, send, _ = call(
        x_finish_kernel, [ybox, (3, 2, subs, lines), (8, lines), xbox],
        ends, other, side, facing, base, lx, rx, dy, wy, cy, name="x_finish",
    )
    ring = [
        lax.ppermute(send, "gy", [(i, (i + back) % columns) for i in range(columns)])
        for back in range(1, columns)
    ]
    swept, yd, xc, xi, zlo, zhi = call(
        y_finish_kernel, [box, ybox, (nz, ny), (nz, ny), (nx, ny), (nx, ny)],
        send, *ring, ybase, ups, ly, ry, cy, name="y_finish",
    )
    xc, xi = across(xc), sibling(xi)
    below, above = up(zhi, "gz"), down(zlo, "gz")
    (ydiff,) = call(turn_kernel, [box], yd, name="turn", flops=10**6)
    (out,) = call(final_kernel, [box], swept, ydiff, near_wind, rate, below, above, xc, xi, name="final")
    return out


def solution(mesh):
    in_specs = (P("gz", "gx", "gy"), P(None, "gz", "gx", "gy"), P("gz", "gx", "gy"))
    out_specs = P("gz", "gx", "gy")
    return jax.shard_map(body, mesh=mesh, in_specs=in_specs, out_specs=out_specs, check_vma=False)
```

```python
import functools
import jax
import jax.numpy as jnp
from jax import lax
from jax.experimental import pallas as pl
from jax.experimental.pallas import tpu as pltpu
from jax.sharding import PartitionSpec as P


QUARTER = 0.25
VERTICAL = 0.06
VMEM_BYTES = 24 * 2**20


def call(kernel, outs, *ins, name, flops=0, scratch=(), far_in=(), far_out=(), alias=None):
    shapes = [jax.ShapeDtypeStruct(s, jnp.float32) for s in outs]
    vm = pl.BlockSpec(memory_space=pltpu.VMEM)
    far = pl.BlockSpec(memory_space=pl.ANY)
    size = 4 * (sum(x.size for x in ins) + sum(x.size for x in shapes))
    return pl.pallas_call(
        kernel,
        out_shape=shapes,
        in_specs=[far if n in far_in else vm for n in range(len(ins))],
        out_specs=[far if n in far_out else vm for n in range(len(outs))],
        scratch_shapes=list(scratch),
        input_output_aliases=alias or {},
        compiler_params=pltpu.CompilerParams(vmem_limit_bytes=VMEM_BYTES),
        cost_estimate=pl.CostEstimate(flops=flops, bytes_accessed=size, transcendentals=0),
        name=name,
    )(*ins)


def merge(a, b):
    a0, a1, aL, aC, aR = a
    b0, b1, bL, bC, bR = b
    inv = 1.0 / (1.0 - aR * bL)
    x = aC * inv
    y = bC * inv
    return (
        a0 + x * (b0 + bL * a1),
        b1 + y * (a1 + aR * b0),
        aL + x * bL * aC,
        x * bC,
        bR + y * aR * bC,
    )


def close_left(p, g, block):
    b0, b1, bL, bC, bR = block
    f = bC / (1.0 - bL * g)
    return b1 + bC * p + f * g * (b0 + bL * p), bR + f * g * bC


def close_right(p, g, block):
    b0, b1, bL, bC, bR = block
    f = bC / (1.0 - bR * g)
    return b0 + bC * p + f * g * (b1 + bR * p), bL + f * g * bC


def chain_ends(blocks, index):
    zero = jnp.zeros_like(blocks[0][0])
    p, g = zero, zero
    lp, lg = zero, zero
    for m in range(len(blocks) - 1):
        p, g = close_left(p, g, blocks[m])
        here = index == m + 1
        lp, lg = jnp.where(here, p, lp), jnp.where(here, g, lg)
    p, g = zero, zero
    rp, rg = zero, zero
    for m in range(len(blocks) - 1, 0, -1):
        p, g = close_right(p, g, blocks[m])
        here = index == m - 1
        rp, rg = jnp.where(here, p, rp), jnp.where(here, g, rg)
    return lp, lg, rp, rg


def factor(d_ref, w_ref, l_ref, r_ref, count):
    delta = 1.0 + d_ref[0]
    w = 1.0 / (1.0 + delta)
    w_ref[0] = w
    y = jnp.ones_like(w)
    l_ref[0] = y
    for i in range(1, count):
        y = y * w
        l_ref[i] = y
        delta = d_ref[i] + delta * w
        w = 1.0 / (1.0 + delta)
        w_ref[i] = w
    r = w
    s = w * y
    r_ref[count - 1] = r
    l_ref[count - 1] = s
    for i in range(count - 2, -1, -1):
        w = w_ref[i]
        r = w * r
        s = w * (l_ref[i] + s)
        r_ref[i] = r
        l_ref[i] = s


def sweep(q, w_ref, out_ref, count):
    y = q(0)
    out_ref[0] = y
    for i in range(1, count):
        y = q(i) + w_ref[i - 1] * y
        out_ref[i] = y
    s = w_ref[count - 1] * y
    out_ref[count - 1] = s
    for i in range(count - 2, -1, -1):
        s = w_ref[i] * (out_ref[i] + s)
        out_ref[i] = s


def stencil(z, f, below, above, west, east, ydiff, wind_ref, k):
    count = f.shape[0]
    row = lax.broadcasted_iota(jnp.int32, f.shape, 0)
    e = jnp.where(row == count - 1, east, pltpu.roll(f, count - 1, 0))
    w = jnp.where(row == 0, west, pltpu.roll(f, 1, 0))
    wz = wind_ref[0, z].astype(jnp.float32)
    wx = wind_ref[1, z].astype(jnp.float32)
    wy = wind_ref[2, z].astype(jnp.float32)
    return (
        f
        - QUARTER * (wz * (above - below) + wx * (e - w) + wy * ydiff)
        + VERTICAL * k * (above + below - 2.0 * f)
    )


def body(field, wind, rate):
    nz, nx, ny = field.shape
    lines = nz * nx
    members = lax.axis_size("gx")
    chips = members // 2
    levels = lax.axis_size("gz")
    columns = lax.axis_size("gy")
    reach = nx * members / 8.0
    c = reach * reach
    subs = 8
    steps = ny // subs
    wide = -(-(lines + 2 * nz) // 128) * 128
    order = (1, 3, 2)

    def core():
        return lax.rem(lax.axis_index("gx"), 2)

    def faces_kernel(f_ref, own, give, xc):
        odd = core() == 1
        low, high = f_ref[0], f_ref[nz - 1]
        own[0:nx] = jnp.where(odd, low, high)
        give[0:nx] = jnp.where(odd, high, low)
        flat = f_ref[...].reshape(lines, ny)
        low = flat[:, :128].T[:1]
        high = flat[:, ny - 128 :].T[127:]
        pad = jnp.zeros((7, lines), jnp.float32)
        own[nx : nx + 8] = jnp.concatenate([jnp.where(odd, low, high), pad], axis=0)
        give[nx : nx + 8] = jnp.concatenate([jnp.where(odd, high, low), pad], axis=0)
        xc[...], give[nx + 8 :] = x_faces(f_ref)

    def x_faces(ref):
        odd = core() == 1
        first, last = ref[:, 0, :], ref[:, nx - 1, :]
        return jnp.where(odd, last, first), jnp.where(odd, first, last)

    def both_faces_kernel(own, got, k_ref, f_ref, planes, columns_out, cross_out, inner):
        planes[0:nx] = own[0:nx]
        planes[nx:] = got[0:nx]
        columns_out[0:8] = own[nx:]
        columns_out[8:16] = got[nx : nx + 8]
        cross_out[0] = f_ref[...]
        cross_out[1], inner[...] = x_faces(k_ref)

    def relay_kernel(planes, columns_in, out_ref):
        out_ref[0:nx] = planes[nx:]
        out_ref[nx:] = columns_in[8:16]

    def up(a, axis):
        n = lax.axis_size(axis)
        return lax.ppermute(a, axis, [(i, (i + 1) % n) for i in range(n)])

    def down(a, axis):
        n = lax.axis_size(axis)
        return lax.ppermute(a, axis, [((i + 1) % n, i) for i in range(n)])

    def y_outward(a):
        pairs = []
        for x in range(members):
            for y in range(columns):
                pairs.append((x * columns + y, x * columns + (y + (-1 if x % 2 else 1)) % columns))
        return lax.ppermute(a, ("gx", "gy"), pairs)

    def z_outward(a):
        pairs = []
        for z in range(levels):
            for x in range(members):
                pairs.append((z * members + x, (z + (-1 if x % 2 else 1)) % levels * members + x))
        return lax.ppermute(a, ("gz", "gx"), pairs)

    def across(a):
        return lax.ppermute(a, "gx", [(i, (i + 1 if i % 2 else i - 1) % members) for i in range(members)])

    def sibling(a):
        return lax.ppermute(a, "gx", [(i, i ^ 1) for i in range(members)])

    def x_sides(cross, inner):
        odd = core() == 1
        return jnp.where(odd, inner, cross), jnp.where(odd, cross, inner)

    def x_rows(cross, inner):
        index = lax.axis_index("gx")
        west, east = x_sides(cross, inner)
        return jnp.where(index == 0, 0.0, west), jnp.where(index == members - 1, 0.0, east)

    def z_planes(below, above):
        index = lax.axis_index("gz")
        return jnp.where(index == 0, 0.0, below), jnp.where(index == levels - 1, 0.0, above)

    def x_matrix_kernel(k_ref, d_ref, w_ref, l_ref, r_ref):
        d_ref[...] = 1.0 / (c * jnp.swapaxes(k_ref[...], 0, 1))
        factor(d_ref, w_ref, l_ref, r_ref, nx)

    def y_matrix_kernel(x_ref, xc, other_ref, d_ref, w_ref, l_ref, r_ref, c_ref):
        west, east = x_sides(xc[1], other_ref[5])
        d = jnp.concatenate(
            [
                x_ref[...].reshape(lines, ny),
                1.0 / (c * west),
                1.0 / (c * east),
                jnp.ones((wide - lines - 2 * nz, ny), jnp.float32),
            ],
            axis=0,
        )
        d_ref[...] = jnp.swapaxes(d.T.reshape(subs, steps, wide), 0, 1)
        factor(d_ref, w_ref, l_ref, r_ref, steps)
        L, C, R = l_ref[0], r_ref[0], r_ref[steps - 1]
        for level in range(3):
            shift = subs - (1 << level)
            bL, bC, bR = pltpu.roll(L, shift, 0), pltpu.roll(C, shift, 0), pltpu.roll(R, shift, 0)
            inv = 1.0 / (1.0 - R * bL)
            x, y = C * inv, bC * inv
            for n, value in enumerate((x, y, bL, R, bC, inv, R * y)):
                c_ref[level, n] = value
            L, C, R = L + x * bL * C, x * bC, bR + y * R * bC
        for n, value in enumerate((L, C, R)):
            c_ref[3, n] = value
        for n in range(3, 7):
            c_ref[3, n] = jnp.zeros_like(L)

    def explicit_kernel(
        f_ref, wind_ref, k_ref, planes, columns_in, relayed, xc, got, kin, d_ref, w_ref, l_ref, r_ref,
        base_ref, ends_ref, e_ref,
    ):
        west, east = x_rows(xc[0], got[nx + 8 :])
        odd = core() == 1
        low, high = z_planes(*choose(odd, (relayed[0:nx], planes[0:nx]), (planes[0:nx], relayed[0:nx])))
        gy = lax.axis_index("gy")
        near, far = columns_in[0:1], relayed[nx : nx + 1]
        left = jnp.where(gy == 0, 0.0, jnp.where(odd, far, near))
        right = jnp.where(gy == columns - 1, 0.0, jnp.where(odd, near, far))
        left = jnp.broadcast_to(left, (128, lines)).T
        right = jnp.broadcast_to(right, (128, lines)).T
        lane = lax.broadcasted_iota(jnp.int32, (nx, 128), 1)
        for z in range(nz):
            f = f_ref[z]
            rows = slice(z * nx, (z + 1) * nx)
            no = pltpu.roll(f, ny - 1, 1)
            so = pltpu.roll(f, 1, 1)
            no = jnp.concatenate([no[:, : ny - 128], jnp.where(lane == 127, right[rows], no[:, ny - 128 :])], axis=1)
            so = jnp.concatenate([jnp.where(lane == 0, left[rows], so[:, :128]), so[:, 128:]], axis=1)
            e_ref[z] = stencil(
                z, f,
                f_ref[z - 1] if z else low,
                f_ref[z + 1] if z < nz - 1 else high,
                west[z : z + 1], east[z : z + 1], no - so, wind_ref, k_ref[z],
            )
        e = jnp.swapaxes(e_ref[...], 0, 1)
        sweep(lambda i: e[i] * d_ref[i], w_ref, base_ref, nx)
        ends = (base_ref[0], base_ref[nx - 1], l_ref[0], r_ref[0], r_ref[nx - 1], kin[...])
        for n, v in enumerate(ends):
            ends_ref[n] = v

    def read(ref):
        return tuple(ref[n] for n in range(5))

    def choose(test, a, b):
        return tuple(jnp.where(test, x, y) for x, y in zip(a, b))

    def ordered(own_ref, got_ref, own_first):
        own, got = read(own_ref), read(got_ref)
        return choose(own_first, own, got), choose(own_first, got, own)

    def chip_kernel(own_ref, got_ref, out_ref):
        b0, b1, L, C, R = merge(*ordered(own_ref, got_ref, core() == 0))
        chip = lax.axis_index("gx") // 2
        first, last = chip == 0, chip == chips - 1
        L, R = jnp.where(first, 0.0, L), jnp.where(last, 0.0, R)
        C = jnp.where(jnp.logical_or(first, last), 0.0, C)
        for n, v in enumerate((b0, b1, L, C, R)):
            out_ref[n] = v

    def pair_kernel(own_ref, got_ref, out_ref):
        for n, v in enumerate(merge(*ordered(own_ref, got_ref, core() == 1))):
            out_ref[n] = v

    def side_kernel(near_ref, far_ref, opposite_ref, out_ref):
        three = merge(*ordered(near_ref, far_ref, core() == 1))
        four = merge(read(opposite_ref), three)
        for n, v in enumerate(choose(core() == 0, four, three)):
            out_ref[n] = v

    def x_finish_kernel(
        ends_ref, other_ref, side_ref, got_ref, base_ref, l_ref, r_ref, d_ref, w_ref, c_ref,
        ybase_ref, up_ref, send_ref, s_ref,
    ):
        odd = core() == 1
        chip = lax.axis_index("gx") // 2
        a, b = ordered(ends_ref, other_ref, core() == 0)
        left, right = ordered(side_ref, got_ref, core() == 0)
        zero = jnp.zeros_like(a[0])
        lp, lg = zero, zero
        for block in (right, left):
            lp, lg = close_left(lp, lg, block)
        rp, rg = zero, zero
        for block in (left, right):
            rp, rg = close_right(rp, rg, block)
        lp, lg = jnp.where(chip == 0, 0.0, lp), jnp.where(chip == 0, 0.0, lg)
        rp, rg = jnp.where(chip == chips - 1, 0.0, rp), jnp.where(chip == chips - 1, 0.0, rg)
        ap, ag = close_left(lp, lg, a)
        bp, bg = close_right(rp, rg, b)
        last_a = (ap + ag * bp) / (1.0 - ag * bg)
        first_b = bp + bg * last_a
        first_a = (a[0] + a[2] * lp + a[3] * first_b) / (1.0 - a[2] * lg)
        last_b = (b[1] + b[4] * rp + b[3] * last_a) / (1.0 - b[4] * rg)
        before = jnp.where(odd, last_a, lp + lg * first_a)
        after = jnp.where(odd, rp + rg * last_b, first_b)
        for i in range(nx):
            s_ref[i] = base_ref[i] + l_ref[i] * before + r_ref[i] * after
        s_ref[nx], s_ref[nx + 1] = before, after
        for i in range(nx + 2, wide // nz):
            s_ref[i] = zero
        t = s_ref[...].reshape(wide, ny).T
        q = jnp.swapaxes(t.reshape(subs, steps, wide), 0, 1)
        sweep(lambda i: q[i] * d_ref[i], w_ref, ybase_ref, steps)
        b0, b1 = ybase_ref[0], ybase_ref[steps - 1]
        for level in range(3):
            shift = subs - (1 << level)
            o0, o1 = pltpu.roll(b0, shift, 0), pltpu.roll(b1, shift, 0)
            x, y, bL, aR, _, inv, _ = (c_ref[level, n] for n in range(7))
            inner = b1 + aR * o0
            up_ref[level, 0] = inner * inv
            up_ref[level, 1] = o0
            b0, b1 = b0 + x * (o0 + bL * b1), o1 + y * inner
        for n, v in enumerate((b0, b1, c_ref[3, 0], c_ref[3, 1], c_ref[3, 2])):
            send_ref[n : n + 1] = v[0:1]
        send_ref[5:8] = jnp.zeros((3, wide), jnp.float32)

    def y_finish_kernel(
        own_ref, *refs,
    ):
        got, (ybase_ref, up_ref, l_ref, r_ref, c_ref), (s_ref, t_ref, ends_ref, west, east, zlo, zhi) = (
            refs[: columns - 1], refs[columns - 1 : columns + 4], refs[columns + 4 :],
        )
        index = lax.axis_index("gy")
        messages = {0: own_ref[...]} | {back: ref[...] for back, ref in zip(order, got)}
        blocks = []
        for m in range(columns):
            v = messages[0]
            for back in range(1, columns):
                v = jnp.where(lax.rem(index - m + columns, columns) == back, messages[back], v)
            blocks.append(tuple(v[n : n + 1] for n in range(5)))
        mine = tuple(messages[0][n : n + 1] for n in range(5))
        lp, lg, rp, rg = chain_ends(blocks, index)
        p, g = close_left(lp, lg, mine)
        last = (p + g * rp) / (1.0 - g * rg)
        right = rp + rg * last
        first = (mine[0] + mine[2] * lp + mine[3] * right) / (1.0 - mine[2] * lg)
        left = lp + lg * first
        sub = lax.broadcasted_iota(jnp.int32, (subs, wide), 0)
        L = jnp.broadcast_to(left, (subs, wide))
        R = jnp.broadcast_to(right, (subs, wide))
        for level in (2, 1, 0):
            step = 1 << level
            x, _, bL, _, bC, _, z = (c_ref[level, n] for n in range(7))
            a = up_ref[level, 0] + x * L + z * R
            b = up_ref[level, 1] + bL * a + bC * R
            upper = (sub & step) != 0
            L, R = (
                jnp.where(upper, pltpu.roll(a, step, 0), L),
                jnp.where(upper, pltpu.roll(R, step, 0), b),
            )
        ends_ref[...] = jnp.concatenate([left, right], axis=0)
        for i in range(steps):
            t_ref[i] = ybase_ref[i] + l_ref[i] * L + r_ref[i] * R
        for first in range(0, wide, 128):
            t = by_rows(t_ref, first).T
            if first < lines:
                rows = slice(first // nz, (first + 128) // nz)
                s_ref[:, rows, :] = jnp.swapaxes(t.reshape(128 // nz, nz, ny), 0, 1)
            else:
                west[...] = t[:nz]
                east[...] = t[nz : 2 * nz]
        zlo[...] = s_ref[0]
        zhi[...] = s_ref[nz - 1]

    def by_rows(ref, first):
        return jnp.swapaxes(ref[:, :, first : first + 128], 0, 1).reshape(ny, 128)

    def inner_kernel(
        t_ref, ends_ref, s_ref, wind_ref, k_ref, west, east, out_ref, edge_ref, factor_ref, yd_ref, buffer, sems
    ):
        for first in range(0, lines, 128):
            s = by_rows(t_ref, first)
            left, right = (ends_ref[n : n + 1, first : first + 128] for n in range(2))
            row = lax.broadcasted_iota(jnp.int32, s.shape, 0)
            north = jnp.where(row == ny - 1, right, pltpu.roll(s, ny - 1, 0))
            south = jnp.where(row == 0, left, pltpu.roll(s, 1, 0))
            rows = slice(first // nz, (first + 128) // nz)
            yd_ref[:, rows, :] = jnp.swapaxes((north - south).T.reshape(128 // nz, nz, ny), 0, 1)
        none = jnp.zeros((nx, ny), jnp.float32)
        copies = []
        for z in range(nz):
            value = stencil(
                z, s_ref[z],
                s_ref[z - 1] if z else none,
                s_ref[z + 1] if z < nz - 1 else none,
                west[z : z + 1], east[z : z + 1], yd_ref[z], wind_ref, k_ref[z],
            )
            if 0 < z < nz - 1:
                buffer[z - 1] = value
                copies.append(pltpu.make_async_copy(buffer.at[z - 1], out_ref.at[z], sems.at[z - 1]))
                copies[-1].start()
            else:
                n = 1 if z else 0
                edge_ref[n] = value
                lift = QUARTER * wind_ref[0, z].astype(jnp.float32)
                factor_ref[n] = VERTICAL * k_ref[z] + (-lift if n else lift)
        for copy in copies:
            copy.wait()

    def final_kernel(part_ref, edge_ref, factor_ref, first, second, out_ref, buffer, sems):
        low, high = z_planes(first[...], second[...])
        buffer[0] = edge_ref[0] + factor_ref[0] * low
        buffer[1] = edge_ref[1] + factor_ref[1] * high
        copies = [pltpu.make_async_copy(buffer.at[n], out_ref.at[z], sems.at[n]) for n, z in enumerate((0, nz - 1))]
        for copy in copies:
            copy.start()
        for copy in copies:
            copy.wait()

    box, xbox, ybox = (nz, nx, ny), (nx, nz, ny), (steps, subs, wide)
    five = (5, nz, ny)

    def outward(a, distance):
        move = lambda i: ((i // 2 + (-distance if i % 2 else distance)) % chips) * 2 + i % 2
        return lax.ppermute(a, "gx", [(i, move(i)) for i in range(members)])

    own, give, xc = call(
        faces_kernel, [(nx + 8, ny), (nx + 8 + nz, ny), (nz, ny)], field, name="faces", flops=10**10
    )
    got = sibling(give)
    planes, edges, xc, kin = call(
        both_faces_kernel, [(2 * nx, ny), (16, lines), (2, nz, ny), (nz, ny)], own, got, rate, xc, name="both_faces"
    )
    planes, edges = z_outward(planes), y_outward(edges)
    (relay,) = call(relay_kernel, [(nx + 8, ny)], planes, edges, name="relay")
    relayed = sibling(relay)
    xc = across(xc)
    dx, wx, lx, rx = call(x_matrix_kernel, [xbox] * 4, rate, name="x_matrix", flops=5 * 10**9)
    base, ends = call(
        explicit_kernel, [xbox, (6, nz, ny)],
        field, wind, rate, planes, edges, relayed, xc, got, kin, dx, wx, lx, rx, name="explicit",
        scratch=[pltpu.VMEM(box, jnp.float32)],
    )
    other = sibling(ends)
    dy, wy, ly, ry, cy = call(
        y_matrix_kernel, [ybox] * 4 + [(4, 7, subs, wide)], dx, xc, other, name="y_matrix", flops=10**6
    )
    (chip,) = call(chip_kernel, [five], ends, other, name="chip")
    opposite = outward(chip, chips // 2)
    near = outward(chip, 1)
    (pair,) = call(pair_kernel, [five], chip, near, name="pair")
    distant = outward(pair, 2)
    (side,) = call(side_kernel, [five], near, distant, opposite, name="side")
    facing = sibling(side)
    ybase, ups, send = call(
        x_finish_kernel, [ybox, (3, 2, subs, wide), (8, wide)],
        ends, other, side, facing, base, lx, rx, dy, wy, cy, name="x_finish",
        scratch=[pltpu.VMEM((wide // nz, nz, ny), jnp.float32)],
    )
    ring = [
        lax.ppermute(send, "gy", [(i, (i + back) % columns) for i in range(columns)])
        for back in order
    ]
    swept, turned, sides, west, east, zlo, zhi = call(
        y_finish_kernel, [box, ybox, (2, wide), (nz, ny), (nz, ny), (nx, ny), (nx, ny)],
        send, *ring, ybase, ups, ly, ry, cy, name="y_finish",
    )
    below, above = up(zhi, "gz"), down(zlo, "gz")
    plane_pair = (2, nx, ny)
    part, edge, factors = call(
        inner_kernel, [box, plane_pair, plane_pair],
        turned, sides, swept, wind, rate, west, east, name="inner", flops=5 * 10**9, far_out=(0,),
        scratch=[
            pltpu.VMEM(box, jnp.float32),
            pltpu.VMEM((nz - 2, nx, ny), jnp.float32),
            pltpu.SemaphoreType.DMA((nz - 2,)),
        ],
    )
    (out,) = call(
        final_kernel, [box], part, edge, factors, below, above, name="final", far_in=(0,), far_out=(0,), alias={0: 0},
        scratch=[pltpu.VMEM(plane_pair, jnp.float32), pltpu.SemaphoreType.DMA((2,))],
    )
    return out


def solution(mesh):
    in_specs = (P("gz", "gx", "gy"), P(None, "gz", "gx", "gy"), P("gz", "gx", "gy"))
    out_specs = P("gz", "gx", "gy")
    return jax.shard_map(body, mesh=mesh, in_specs=in_specs, out_specs=out_specs, check_vma=False)
```

```python
import functools
import jax
import jax.numpy as jnp
from jax import lax
from jax.experimental import pallas as pl
from jax.experimental.pallas import tpu as pltpu
from jax.sharding import PartitionSpec as P


QUARTER = 0.25
VERTICAL = 0.06
VMEM_BYTES = 24 * 2**20


def call(kernel, outs, *ins, name, flops=0, scratch=(), far_in=(), far_out=(), alias=None):
    shapes = [jax.ShapeDtypeStruct(s, jnp.float32) for s in outs]
    vm = pl.BlockSpec(memory_space=pltpu.VMEM)
    far = pl.BlockSpec(memory_space=pl.ANY)
    size = 4 * (sum(x.size for x in ins) + sum(x.size for x in shapes))
    return pl.pallas_call(
        kernel,
        out_shape=shapes,
        in_specs=[far if n in far_in else vm for n in range(len(ins))],
        out_specs=[far if n in far_out else vm for n in range(len(outs))],
        scratch_shapes=list(scratch),
        input_output_aliases=alias or {},
        compiler_params=pltpu.CompilerParams(vmem_limit_bytes=VMEM_BYTES),
        cost_estimate=pl.CostEstimate(flops=flops, bytes_accessed=size, transcendentals=0),
        name=name,
    )(*ins)


def merge(a, b):
    a0, a1, aL, aC, aR = a
    b0, b1, bL, bC, bR = b
    inv = 1.0 / (1.0 - aR * bL)
    x = aC * inv
    y = bC * inv
    return (
        a0 + x * (b0 + bL * a1),
        b1 + y * (a1 + aR * b0),
        aL + x * bL * aC,
        x * bC,
        bR + y * aR * bC,
    )


def close_left(p, g, block):
    b0, b1, bL, bC, bR = block
    f = bC / (1.0 - bL * g)
    return b1 + bC * p + f * g * (b0 + bL * p), bR + f * g * bC


def close_right(p, g, block):
    b0, b1, bL, bC, bR = block
    f = bC / (1.0 - bR * g)
    return b0 + bC * p + f * g * (b1 + bR * p), bL + f * g * bC


def chain_ends(blocks, index):
    zero = jnp.zeros_like(blocks[0][0])
    p, g = zero, zero
    lp, lg = zero, zero
    for m in range(len(blocks) - 1):
        p, g = close_left(p, g, blocks[m])
        here = index == m + 1
        lp, lg = jnp.where(here, p, lp), jnp.where(here, g, lg)
    p, g = zero, zero
    rp, rg = zero, zero
    for m in range(len(blocks) - 1, 0, -1):
        p, g = close_right(p, g, blocks[m])
        here = index == m - 1
        rp, rg = jnp.where(here, p, rp), jnp.where(here, g, rg)
    return lp, lg, rp, rg


def factor(d_ref, w_ref, l_ref, r_ref, count):
    delta = 1.0 + d_ref[0]
    w = 1.0 / (1.0 + delta)
    w_ref[0] = w
    y = jnp.ones_like(w)
    l_ref[0] = y
    for i in range(1, count):
        y = y * w
        l_ref[i] = y
        delta = d_ref[i] + delta * w
        w = 1.0 / (1.0 + delta)
        w_ref[i] = w
    r = w
    s = w * y
    r_ref[count - 1] = r
    l_ref[count - 1] = s
    for i in range(count - 2, -1, -1):
        w = w_ref[i]
        r = w * r
        s = w * (l_ref[i] + s)
        r_ref[i] = r
        l_ref[i] = s


def sweep(q, w_ref, out_ref, count):
    y = q(0)
    out_ref[0] = y
    for i in range(1, count):
        y = q(i) + w_ref[i - 1] * y
        out_ref[i] = y
    s = w_ref[count - 1] * y
    out_ref[count - 1] = s
    for i in range(count - 2, -1, -1):
        s = w_ref[i] * (out_ref[i] + s)
        out_ref[i] = s


def stencil(z, f, below, above, west, east, ydiff, wind_ref, k):
    count = f.shape[0]
    row = lax.broadcasted_iota(jnp.int32, f.shape, 0)
    e = jnp.where(row == count - 1, east, pltpu.roll(f, count - 1, 0))
    w = jnp.where(row == 0, west, pltpu.roll(f, 1, 0))
    wz = wind_ref[0, z].astype(jnp.float32)
    wx = wind_ref[1, z].astype(jnp.float32)
    wy = wind_ref[2, z].astype(jnp.float32)
    return (
        f
        - QUARTER * (wz * (above - below) + wx * (e - w) + wy * ydiff)
        + VERTICAL * k * (above + below - 2.0 * f)
    )


def body(field, wind, rate):
    nz, nx, ny = field.shape
    lines = nz * nx
    members = lax.axis_size("gx")
    chips = members // 2
    levels = lax.axis_size("gz")
    columns = lax.axis_size("gy")
    reach = nx * members / 8.0
    c = reach * reach
    subs = 8
    steps = ny // subs
    wide = -(-(lines + 2 * nz) // 128) * 128
    order = (1, 3, 2)

    def core():
        return lax.rem(lax.axis_index("gx"), 2)

    def faces_kernel(f_ref, own, give, xc):
        odd = core() == 1
        low, high = f_ref[0], f_ref[nz - 1]
        own[0:nx] = jnp.where(odd, high, low)
        give[0:nx] = jnp.where(odd, low, high)
        flat = f_ref[...].reshape(lines, ny)
        low = flat[:, :128].T[:1]
        high = flat[:, ny - 128 :].T[127:]
        pad = jnp.zeros((7, lines), jnp.float32)
        own[nx : nx + 8] = jnp.concatenate([jnp.where(odd, high, low), pad], axis=0)
        give[nx : nx + 8] = jnp.concatenate([jnp.where(odd, low, high), pad], axis=0)
        xc[0:nz], give[nx + 8 :] = x_faces(f_ref)

    def x_faces(ref):
        odd = core() == 1
        first, last = ref[:, 0, :], ref[:, nx - 1, :]
        return jnp.where(odd, last, first), jnp.where(odd, first, last)

    def both_faces_kernel(own, got, planes, columns_out):
        planes[0:nx] = got[0:nx]
        planes[nx:] = own[0:nx]
        columns_out[0:8] = got[nx : nx + 8]
        columns_out[8:16] = own[nx:]

    def relay_kernel(planes, columns_in, out_ref):
        out_ref[0:nx] = planes[nx:]
        out_ref[nx:] = columns_in[8:16]

    def y_outward(a):
        pairs = []
        for x in range(members):
            for y in range(columns):
                pairs.append((x * columns + y, (x ^ 1) * columns + (y + (1 if x % 2 else -1)) % columns))
        return lax.ppermute(a, ("gx", "gy"), pairs)

    def z_outward(a):
        pairs = []
        for z in range(levels):
            for x in range(members):
                to = z + (1 if x % 2 else -1)
                pairs.append((z * members + x, to * members + (x ^ 1) if 0 <= to < levels else z * members + (x ^ 2)))
        return lax.ppermute(a, ("gz", "gx"), pairs)

    def z_swap(a, parity):
        pairs = []
        for z in range(levels):
            for x in range(members):
                to = z + (1 if z % 2 == parity else -1)
                pairs.append((z * members + x, to * members + x if 0 <= to < levels else z * members + (x ^ 1)))
        return lax.ppermute(a, ("gz", "gx"), pairs)

    def z_order(low, high):
        even = lax.rem(lax.axis_index("gz"), 2) == 0
        return jnp.where(even, high, low), jnp.where(even, low, high)

    def across(a):
        return lax.ppermute(a, "gx", [(i, (i + 1 if i % 2 else i - 1) % members) for i in range(members)])

    def sibling(a):
        return lax.ppermute(a, "gx", [(i, i ^ 1) for i in range(members)])

    def x_sides(cross, inner):
        odd = core() == 1
        return jnp.where(odd, inner, cross), jnp.where(odd, cross, inner)

    def x_rows(cross, inner):
        index = lax.axis_index("gx")
        west, east = x_sides(cross, inner)
        return jnp.where(index == 0, 0.0, west), jnp.where(index == members - 1, 0.0, east)

    def z_planes(below, above):
        index = lax.axis_index("gz")
        return jnp.where(index == 0, 0.0, below), jnp.where(index == levels - 1, 0.0, above)

    def x_matrix_kernel(k_ref, d_ref, w_ref, l_ref, r_ref):
        d_ref[...] = 1.0 / (c * jnp.swapaxes(k_ref[...], 0, 1))
        factor(d_ref, w_ref, l_ref, r_ref, nx)

    def y_matrix_kernel(x_ref, near_ref, other_ref, d_ref, w_ref, l_ref, r_ref, c_ref):
        west, east = x_sides(near_ref[5], other_ref[6])
        d = jnp.concatenate(
            [
                x_ref[...].reshape(lines, ny),
                1.0 / (c * west),
                1.0 / (c * east),
                jnp.ones((wide - lines - 2 * nz, ny), jnp.float32),
            ],
            axis=0,
        )
        d_ref[...] = jnp.swapaxes(d.T.reshape(subs, steps, wide), 0, 1)
        factor(d_ref, w_ref, l_ref, r_ref, steps)
        L, C, R = l_ref[0], r_ref[0], r_ref[steps - 1]
        for level in range(3):
            shift = subs - (1 << level)
            bL, bC, bR = pltpu.roll(L, shift, 0), pltpu.roll(C, shift, 0), pltpu.roll(R, shift, 0)
            inv = 1.0 / (1.0 - R * bL)
            x, y = C * inv, bC * inv
            for n, value in enumerate((x, y, bL, R, bC, inv, R * y)):
                c_ref[level, n] = value
            L, C, R = L + x * bL * C, x * bC, bR + y * R * bC
        for n, value in enumerate((L, C, R)):
            c_ref[3, n] = value
        for n in range(3, 7):
            c_ref[3, n] = jnp.zeros_like(L)

    def explicit_kernel(
        f_ref, wind_ref, k_ref, planes, columns_in, relayed, xc, got, d_ref, w_ref, l_ref, r_ref,
        base_ref, ends_ref, e_ref,
    ):
        west, east = x_rows(xc[0:nz], got[nx + 8 :])
        odd = core() == 1
        low, high = z_planes(*choose(odd, (relayed[0:nx], planes[0:nx]), (planes[0:nx], relayed[0:nx])))
        gy = lax.axis_index("gy")
        near, far = columns_in[0:1], relayed[nx : nx + 1]
        left = jnp.where(gy == 0, 0.0, jnp.where(odd, far, near))
        right = jnp.where(gy == columns - 1, 0.0, jnp.where(odd, near, far))
        left = jnp.broadcast_to(left, (128, lines)).T
        right = jnp.broadcast_to(right, (128, lines)).T
        lane = lax.broadcasted_iota(jnp.int32, (nx, 128), 1)
        for z in range(nz):
            f = f_ref[z]
            rows = slice(z * nx, (z + 1) * nx)
            no = pltpu.roll(f, ny - 1, 1)
            so = pltpu.roll(f, 1, 1)
            no = jnp.concatenate([no[:, : ny - 128], jnp.where(lane == 127, right[rows], no[:, ny - 128 :])], axis=1)
            so = jnp.concatenate([jnp.where(lane == 0, left[rows], so[:, :128]), so[:, 128:]], axis=1)
            e_ref[z] = stencil(
                z, f,
                f_ref[z - 1] if z else low,
                f_ref[z + 1] if z < nz - 1 else high,
                west[z : z + 1], east[z : z + 1], no - so, wind_ref, k_ref[z],
            )
        e = jnp.swapaxes(e_ref[...], 0, 1)
        sweep(lambda i: e[i] * d_ref[i], w_ref, base_ref, nx)
        ends = (base_ref[0], base_ref[nx - 1], l_ref[0], r_ref[0], r_ref[nx - 1]) + x_faces(k_ref)
        for n, v in enumerate(ends):
            ends_ref[n] = v

    def read(ref):
        return tuple(ref[n] for n in range(5))

    def choose(test, a, b):
        return tuple(jnp.where(test, x, y) for x, y in zip(a, b))

    def ordered(own_ref, got_ref, own_first):
        own, got = read(own_ref), read(got_ref)
        return choose(own_first, own, got), choose(own_first, got, own)

    def chip_kernel(own_ref, got_ref, out_ref, near_ref):
        b0, b1, L, C, R = merge(*ordered(own_ref, got_ref, core() == 0))
        chip = lax.axis_index("gx") // 2
        first, last = chip == 0, chip == chips - 1
        L, R = jnp.where(first, 0.0, L), jnp.where(last, 0.0, R)
        C = jnp.where(jnp.logical_or(first, last), 0.0, C)
        for n, v in enumerate((b0, b1, L, C, R)):
            out_ref[n] = near_ref[n] = v
        near_ref[5] = own_ref[5]

    def pair_kernel(own_ref, got_ref, out_ref):
        for n, v in enumerate(merge(*ordered(own_ref, got_ref, core() == 1))):
            out_ref[n] = v

    def side_kernel(near_ref, far_ref, opposite_ref, out_ref):
        three = merge(*ordered(near_ref, far_ref, core() == 1))
        four = merge(read(opposite_ref), three)
        for n, v in enumerate(choose(core() == 0, four, three)):
            out_ref[n] = v

    def x_finish_kernel(
        ends_ref, other_ref, side_ref, got_ref, base_ref, l_ref, r_ref, d_ref, w_ref, c_ref,
        ybase_ref, up_ref, send_ref, s_ref,
    ):
        odd = core() == 1
        chip = lax.axis_index("gx") // 2
        a, b = ordered(ends_ref, other_ref, core() == 0)
        left, right = ordered(side_ref, got_ref, core() == 0)
        zero = jnp.zeros_like(a[0])
        lp, lg = zero, zero
        for block in (right, left):
            lp, lg = close_left(lp, lg, block)
        rp, rg = zero, zero
        for block in (left, right):
            rp, rg = close_right(rp, rg, block)
        lp, lg = jnp.where(chip == 0, 0.0, lp), jnp.where(chip == 0, 0.0, lg)
        rp, rg = jnp.where(chip == chips - 1, 0.0, rp), jnp.where(chip == chips - 1, 0.0, rg)
        ap, ag = close_left(lp, lg, a)
        bp, bg = close_right(rp, rg, b)
        last_a = (ap + ag * bp) / (1.0 - ag * bg)
        first_b = bp + bg * last_a
        first_a = (a[0] + a[2] * lp + a[3] * first_b) / (1.0 - a[2] * lg)
        last_b = (b[1] + b[4] * rp + b[3] * last_a) / (1.0 - b[4] * rg)
        before = jnp.where(odd, last_a, lp + lg * first_a)
        after = jnp.where(odd, rp + rg * last_b, first_b)
        for i in range(nx):
            s_ref[i] = base_ref[i] + l_ref[i] * before + r_ref[i] * after
        s_ref[nx], s_ref[nx + 1] = before, after
        for i in range(nx + 2, wide // nz):
            s_ref[i] = zero
        t = s_ref[...].reshape(wide, ny).T
        q = jnp.swapaxes(t.reshape(subs, steps, wide), 0, 1)
        sweep(lambda i: q[i] * d_ref[i], w_ref, ybase_ref, steps)
        b0, b1 = ybase_ref[0], ybase_ref[steps - 1]
        for level in range(3):
            shift = subs - (1 << level)
            o0, o1 = pltpu.roll(b0, shift, 0), pltpu.roll(b1, shift, 0)
            x, y, bL, aR, _, inv, _ = (c_ref[level, n] for n in range(7))
            inner = b1 + aR * o0
            up_ref[level, 0] = inner * inv
            up_ref[level, 1] = o0
            b0, b1 = b0 + x * (o0 + bL * b1), o1 + y * inner
        for n, v in enumerate((b0, b1, c_ref[3, 0], c_ref[3, 1], c_ref[3, 2])):
            send_ref[n : n + 1] = v[0:1]
        send_ref[5:8] = jnp.zeros((3, wide), jnp.float32)

    def y_finish_kernel(
        own_ref, *refs,
    ):
        got, (ybase_ref, up_ref, l_ref, r_ref, c_ref), (s_ref, t_ref, ends_ref, west, east, first_plane, second_plane) = (
            refs[: columns - 1], refs[columns - 1 : columns + 4], refs[columns + 4 :],
        )
        index = lax.axis_index("gy")
        messages = {0: own_ref[...]} | {back: ref[...] for back, ref in zip(order, got)}
        blocks = []
        for m in range(columns):
            v = messages[0]
            for back in range(1, columns):
                v = jnp.where(lax.bitwise_xor(index, back) == m, messages[back], v)
            blocks.append(tuple(v[n : n + 1] for n in range(5)))
        mine = tuple(messages[0][n : n + 1] for n in range(5))
        lp, lg, rp, rg = chain_ends(blocks, index)
        p, g = close_left(lp, lg, mine)
        last = (p + g * rp) / (1.0 - g * rg)
        right = rp + rg * last
        first = (mine[0] + mine[2] * lp + mine[3] * right) / (1.0 - mine[2] * lg)
        left = lp + lg * first
        sub = lax.broadcasted_iota(jnp.int32, (subs, wide), 0)
        L = jnp.broadcast_to(left, (subs, wide))
        R = jnp.broadcast_to(right, (subs, wide))
        for level in (2, 1, 0):
            step = 1 << level
            x, _, bL, _, bC, _, z = (c_ref[level, n] for n in range(7))
            a = up_ref[level, 0] + x * L + z * R
            b = up_ref[level, 1] + bL * a + bC * R
            upper = (sub & step) != 0
            L, R = (
                jnp.where(upper, pltpu.roll(a, step, 0), L),
                jnp.where(upper, pltpu.roll(R, step, 0), b),
            )
        ends_ref[...] = jnp.concatenate([left, right], axis=0)
        for i in range(steps):
            t_ref[i] = ybase_ref[i] + l_ref[i] * L + r_ref[i] * R
        for first in range(0, wide, 128):
            t = by_rows(t_ref, first).T
            if first < lines:
                rows = slice(first // nz, (first + 128) // nz)
                s_ref[:, rows, :] = jnp.swapaxes(t.reshape(128 // nz, nz, ny), 0, 1)
            else:
                west[...] = t[:nz]
                east[...] = t[nz : 2 * nz]
        first_plane[...], second_plane[...] = z_order(s_ref[0], s_ref[nz - 1])

    def by_rows(ref, first):
        return jnp.swapaxes(ref[:, :, first : first + 128], 0, 1).reshape(ny, 128)

    def inner_kernel(
        t_ref, ends_ref, s_ref, wind_ref, k_ref, west, east, out_ref, edge_ref, factor_ref, yd_ref, buffer, sems
    ):
        for first in range(0, lines, 128):
            s = by_rows(t_ref, first)
            left, right = (ends_ref[n : n + 1, first : first + 128] for n in range(2))
            row = lax.broadcasted_iota(jnp.int32, s.shape, 0)
            north = jnp.where(row == ny - 1, right, pltpu.roll(s, ny - 1, 0))
            south = jnp.where(row == 0, left, pltpu.roll(s, 1, 0))
            rows = slice(first // nz, (first + 128) // nz)
            yd_ref[:, rows, :] = jnp.swapaxes((north - south).T.reshape(128 // nz, nz, ny), 0, 1)
        none = jnp.zeros((nx, ny), jnp.float32)
        copies = []
        for z in range(nz):
            value = stencil(
                z, s_ref[z],
                s_ref[z - 1] if z else none,
                s_ref[z + 1] if z < nz - 1 else none,
                west[z : z + 1], east[z : z + 1], yd_ref[z], wind_ref, k_ref[z],
            )
            if 0 < z < nz - 1:
                buffer[z - 1] = value
                copies.append(pltpu.make_async_copy(buffer.at[z - 1], out_ref.at[z], sems.at[z - 1]))
                copies[-1].start()
            else:
                n = 1 if z else 0
                edge_ref[n] = value
                lift = QUARTER * wind_ref[0, z].astype(jnp.float32)
                factor_ref[n] = VERTICAL * k_ref[z] + (-lift if n else lift)
        for copy in copies:
            copy.wait()

    def final_kernel(part_ref, edge_ref, factor_ref, first, second, out_ref, buffer, sems):
        low, high = z_planes(*z_order(first[...], second[...]))
        buffer[0] = edge_ref[0] + factor_ref[0] * low
        buffer[1] = edge_ref[1] + factor_ref[1] * high
        copies = [pltpu.make_async_copy(buffer.at[n], out_ref.at[z], sems.at[n]) for n, z in enumerate((0, nz - 1))]
        for copy in copies:
            copy.start()
        for copy in copies:
            copy.wait()

    box, xbox, ybox = (nz, nx, ny), (nx, nz, ny), (steps, subs, wide)
    five = (5, nz, ny)

    def outward(a, distance):
        move = lambda i: ((i // 2 + (-distance if i % 2 else distance)) % chips) * 2 + i % 2
        return lax.ppermute(a, "gx", [(i, move(i)) for i in range(members)])

    own, give, xc = call(
        faces_kernel, [(nx + 8, ny), (nx + 8 + nz, ny), (nz, ny)], field, name="faces", flops=10**10
    )
    got = sibling(give)
    planes, edges = call(both_faces_kernel, [(2 * nx, ny), (16, lines)], own, got, name="both_faces")
    planes, edges = z_outward(planes), y_outward(edges)
    (relay,) = call(relay_kernel, [(nx + 8, ny)], planes, edges, name="relay")
    relayed = sibling(relay)
    xc = across(xc)
    dx, wx, lx, rx = call(x_matrix_kernel, [xbox] * 4, rate, name="x_matrix", flops=5 * 10**9)
    base, ends = call(
        explicit_kernel, [xbox, (7, nz, ny)],
        field, wind, rate, planes, edges, relayed, xc, got, dx, wx, lx, rx, name="explicit",
        scratch=[pltpu.VMEM(box, jnp.float32)],
    )
    other = sibling(ends)
    chip, chip_near = call(chip_kernel, [five, (6, nz, ny)], ends, other, name="chip")
    opposite = outward(chip, chips // 2)
    near = across(chip_near)
    dy, wy, ly, ry, cy = call(
        y_matrix_kernel, [ybox] * 4 + [(4, 7, subs, wide)], dx, near, other, name="y_matrix", flops=10**6
    )
    (pair,) = call(pair_kernel, [five], chip, near, name="pair")
    distant = outward(pair, 2)
    (side,) = call(side_kernel, [five], near, distant, opposite, name="side")
    facing = sibling(side)
    ybase, ups, send = call(
        x_finish_kernel, [ybox, (3, 2, subs, wide), (8, wide)],
        ends, other, side, facing, base, lx, rx, dy, wy, cy, name="x_finish",
        scratch=[pltpu.VMEM((wide // nz, nz, ny), jnp.float32)],
    )
    ring = [
        lax.ppermute(send, "gy", [(i, i ^ back) for i in range(columns)])
        for back in order
    ]
    swept, turned, sides, west, east, first, second = call(
        y_finish_kernel, [box, ybox, (2, wide), (nz, ny), (nz, ny), (nx, ny), (nx, ny)],
        send, *ring, ybase, ups, ly, ry, cy, name="y_finish",
    )
    first, second = z_swap(first, 0), z_swap(second, 1)
    plane_pair = (2, nx, ny)
    part, edge, factors = call(
        inner_kernel, [box, plane_pair, plane_pair],
        turned, sides, swept, wind, rate, west, east, name="inner", flops=5 * 10**9, far_out=(0,),
        scratch=[
            pltpu.VMEM(box, jnp.float32),
            pltpu.VMEM((nz - 2, nx, ny), jnp.float32),
            pltpu.SemaphoreType.DMA((nz - 2,)),
        ],
    )
    (out,) = call(
        final_kernel, [box], part, edge, factors, first, second, name="final", far_in=(0,), far_out=(0,), alias={0: 0},
        scratch=[pltpu.VMEM(plane_pair, jnp.float32), pltpu.SemaphoreType.DMA((2,))],
    )
    return out


def solution(mesh):
    in_specs = (P("gz", "gx", "gy"), P(None, "gz", "gx", "gy"), P("gz", "gx", "gy"))
    out_specs = P("gz", "gx", "gy")
    return jax.shard_map(body, mesh=mesh, in_specs=in_specs, out_specs=out_specs, check_vma=False)
```

```python
import functools
import jax
import jax.numpy as jnp
from jax import lax
from jax.experimental import pallas as pl
from jax.experimental.pallas import tpu as pltpu
from jax.sharding import PartitionSpec as P


QUARTER = 0.25
VERTICAL = 0.06
VMEM_BYTES = 24 * 2**20


def call(kernel, outs, *ins, name, flops=0, scratch=(), far_in=(), far_out=(), alias=None):
    shapes = [jax.ShapeDtypeStruct(s, jnp.float32) for s in outs]
    vm = pl.BlockSpec(memory_space=pltpu.VMEM)
    far = pl.BlockSpec(memory_space=pl.ANY)
    size = 4 * (sum(x.size for x in ins) + sum(x.size for x in shapes))
    return pl.pallas_call(
        kernel,
        out_shape=shapes,
        in_specs=[far if n in far_in else vm for n in range(len(ins))],
        out_specs=[far if n in far_out else vm for n in range(len(outs))],
        scratch_shapes=list(scratch),
        input_output_aliases=alias or {},
        compiler_params=pltpu.CompilerParams(vmem_limit_bytes=VMEM_BYTES),
        cost_estimate=pl.CostEstimate(flops=flops, bytes_accessed=size, transcendentals=0),
        name=name,
    )(*ins)


def merge(a, b):
    a0, a1, aL, aC, aR = a
    b0, b1, bL, bC, bR = b
    inv = 1.0 / (1.0 - aR * bL)
    x = aC * inv
    y = bC * inv
    return (
        a0 + x * (b0 + bL * a1),
        b1 + y * (a1 + aR * b0),
        aL + x * bL * aC,
        x * bC,
        bR + y * aR * bC,
    )


def close_left(p, g, block):
    b0, b1, bL, bC, bR = block
    f = bC / (1.0 - bL * g)
    return b1 + bC * p + f * g * (b0 + bL * p), bR + f * g * bC


def close_right(p, g, block):
    b0, b1, bL, bC, bR = block
    f = bC / (1.0 - bR * g)
    return b0 + bC * p + f * g * (b1 + bR * p), bL + f * g * bC


def chain_ends(blocks, index):
    zero = jnp.zeros_like(blocks[0][0])
    p, g = zero, zero
    lp, lg = zero, zero
    for m in range(len(blocks) - 1):
        p, g = close_left(p, g, blocks[m])
        here = index == m + 1
        lp, lg = jnp.where(here, p, lp), jnp.where(here, g, lg)
    p, g = zero, zero
    rp, rg = zero, zero
    for m in range(len(blocks) - 1, 0, -1):
        p, g = close_right(p, g, blocks[m])
        here = index == m - 1
        rp, rg = jnp.where(here, p, rp), jnp.where(here, g, rg)
    return lp, lg, rp, rg


def factor(d_ref, w_ref, l_ref, r_ref, count):
    delta = 1.0 + d_ref[0]
    w = 1.0 / (1.0 + delta)
    w_ref[0] = w
    y = jnp.ones_like(w)
    l_ref[0] = y
    for i in range(1, count):
        y = y * w
        l_ref[i] = y
        delta = d_ref[i] + delta * w
        w = 1.0 / (1.0 + delta)
        w_ref[i] = w
    r = w
    s = w * y
    r_ref[count - 1] = r
    l_ref[count - 1] = s
    for i in range(count - 2, -1, -1):
        w = w_ref[i]
        r = w * r
        s = w * (l_ref[i] + s)
        r_ref[i] = r
        l_ref[i] = s


def sweep(q, w_ref, out_ref, count):
    y = q(0)
    out_ref[0] = y
    for i in range(1, count):
        y = q(i) + w_ref[i - 1] * y
        out_ref[i] = y
    s = w_ref[count - 1] * y
    out_ref[count - 1] = s
    for i in range(count - 2, -1, -1):
        s = w_ref[i] * (out_ref[i] + s)
        out_ref[i] = s


def stencil(z, f, below, above, west, east, ydiff, wind_ref, k):
    count = f.shape[0]
    row = lax.broadcasted_iota(jnp.int32, f.shape, 0)
    e = jnp.where(row == count - 1, east, pltpu.roll(f, count - 1, 0))
    w = jnp.where(row == 0, west, pltpu.roll(f, 1, 0))
    wz = wind_ref[0, z].astype(jnp.float32)
    wx = wind_ref[1, z].astype(jnp.float32)
    wy = wind_ref[2, z].astype(jnp.float32)
    return (
        f
        - QUARTER * (wz * (above - below) + wx * (e - w) + wy * ydiff)
        + VERTICAL * k * (above + below - 2.0 * f)
    )


def body(field, wind, rate):
    nz, nx, ny = field.shape
    lines = nz * nx
    members = lax.axis_size("gx")
    chips = members // 2
    levels = lax.axis_size("gz")
    columns = lax.axis_size("gy")
    reach = nx * members / 8.0
    c = reach * reach
    subs = 8
    steps = ny // subs
    wide = -(-(lines + 2 * nz) // 128) * 128
    order = (1, 3, 2)

    def core():
        return lax.rem(lax.axis_index("gx"), 2)

    def faces_kernel(f_ref, own, give, xc):
        odd = core() == 1
        low, high = f_ref[0], f_ref[nz - 1]
        own[0:nx] = jnp.where(odd, high, low)
        give[0:nx] = jnp.where(odd, low, high)
        flat = f_ref[...].reshape(lines, ny)
        low = flat[:, :128].T[:1]
        high = flat[:, ny - 128 :].T[127:]
        pad = jnp.zeros((7, lines), jnp.float32)
        own[nx : nx + 8] = jnp.concatenate([jnp.where(odd, high, low), pad], axis=0)
        give[nx : nx + 8] = jnp.concatenate([jnp.where(odd, low, high), pad], axis=0)
        xc[0:nz], give[nx + 8 :] = x_faces(f_ref)

    def x_faces(ref):
        odd = core() == 1
        first, last = ref[:, 0, :], ref[:, nx - 1, :]
        return jnp.where(odd, last, first), jnp.where(odd, first, last)

    def both_faces_kernel(own, got, planes, columns_out):
        planes[0:nx] = got[0:nx]
        planes[nx:] = own[0:nx]
        columns_out[0:8] = got[nx : nx + 8]
        columns_out[8:16] = own[nx:]

    def relay_kernel(planes, columns_in, out_ref):
        out_ref[0:nx] = planes[nx:]
        out_ref[nx:] = columns_in[8:16]

    def y_outward(a):
        pairs = []
        for x in range(members):
            for y in range(columns):
                pairs.append((x * columns + y, (x ^ 1) * columns + (y + (1 if x % 2 else -1)) % columns))
        return lax.ppermute(a, ("gx", "gy"), pairs)

    def z_outward(a):
        pairs = []
        for z in range(levels):
            for x in range(members):
                to = z + (1 if x % 2 else -1)
                pairs.append((z * members + x, to * members + (x ^ 1) if 0 <= to < levels else z * members + (x ^ 2)))
        return lax.ppermute(a, ("gz", "gx"), pairs)

    def z_swap(a, parity):
        pairs = []
        for z in range(levels):
            for x in range(members):
                to = z + (1 if z % 2 == parity else -1)
                pairs.append((z * members + x, to * members + x if 0 <= to < levels else z * members + (x ^ 1)))
        return lax.ppermute(a, ("gz", "gx"), pairs)

    def z_order(low, high):
        even = lax.rem(lax.axis_index("gz"), 2) == 0
        return jnp.where(even, high, low), jnp.where(even, low, high)

    def across(a):
        return lax.ppermute(a, "gx", [(i, (i + 1 if i % 2 else i - 1) % members) for i in range(members)])

    def sibling(a):
        return lax.ppermute(a, "gx", [(i, i ^ 1) for i in range(members)])

    def x_sides(cross, inner):
        odd = core() == 1
        return jnp.where(odd, inner, cross), jnp.where(odd, cross, inner)

    def x_rows(cross, inner):
        index = lax.axis_index("gx")
        west, east = x_sides(cross, inner)
        return jnp.where(index == 0, 0.0, west), jnp.where(index == members - 1, 0.0, east)

    def z_planes(below, above):
        index = lax.axis_index("gz")
        return jnp.where(index == 0, 0.0, below), jnp.where(index == levels - 1, 0.0, above)

    def x_matrix_kernel(k_ref, d_ref, w_ref, l_ref, r_ref):
        d_ref[...] = 1.0 / (c * jnp.swapaxes(k_ref[...], 0, 1))
        factor(d_ref, w_ref, l_ref, r_ref, nx)

    def y_matrix_kernel(x_ref, near_ref, other_ref, d_ref, w_ref, l_ref, r_ref, c_ref):
        west, east = x_sides(near_ref[5], other_ref[6])
        d = jnp.concatenate(
            [
                x_ref[...].reshape(lines, ny),
                1.0 / (c * west),
                1.0 / (c * east),
                jnp.ones((wide - lines - 2 * nz, ny), jnp.float32),
            ],
            axis=0,
        )
        d_ref[...] = jnp.swapaxes(d.T.reshape(subs, steps, wide), 0, 1)
        factor(d_ref, w_ref, l_ref, r_ref, steps)
        L, C, R = l_ref[0], r_ref[0], r_ref[steps - 1]
        for level in range(3):
            shift = subs - (1 << level)
            bL, bC, bR = pltpu.roll(L, shift, 0), pltpu.roll(C, shift, 0), pltpu.roll(R, shift, 0)
            inv = 1.0 / (1.0 - R * bL)
            x, y = C * inv, bC * inv
            for n, value in enumerate((x, y, bL, R, bC, inv, R * y)):
                c_ref[level, n] = value
            L, C, R = L + x * bL * C, x * bC, bR + y * R * bC
        for n, value in enumerate((L, C, R)):
            c_ref[3, n] = value
        for n in range(3, 7):
            c_ref[3, n] = jnp.zeros_like(L)

    def explicit_kernel(
        f_ref, wind_ref, k_ref, planes, columns_in, relayed, xc, got, d_ref, w_ref, l_ref, r_ref,
        base_ref, ends_ref, e_ref,
    ):
        west, east = x_rows(xc[0:nz], got[nx + 8 :])
        odd = core() == 1
        low, high = z_planes(*choose(odd, (relayed[0:nx], planes[0:nx]), (planes[0:nx], relayed[0:nx])))
        gy = lax.axis_index("gy")
        near, far = columns_in[0:1], relayed[nx : nx + 1]
        left = jnp.where(gy == 0, 0.0, jnp.where(odd, far, near))
        right = jnp.where(gy == columns - 1, 0.0, jnp.where(odd, near, far))
        left = jnp.broadcast_to(left, (128, lines)).T
        right = jnp.broadcast_to(right, (128, lines)).T
        lane = lax.broadcasted_iota(jnp.int32, (nx, 128), 1)
        for z in range(nz):
            f = f_ref[z]
            rows = slice(z * nx, (z + 1) * nx)
            no = pltpu.roll(f, ny - 1, 1)
            so = pltpu.roll(f, 1, 1)
            no = jnp.concatenate([no[:, : ny - 128], jnp.where(lane == 127, right[rows], no[:, ny - 128 :])], axis=1)
            so = jnp.concatenate([jnp.where(lane == 0, left[rows], so[:, :128]), so[:, 128:]], axis=1)
            e_ref[z] = stencil(
                z, f,
                f_ref[z - 1] if z else low,
                f_ref[z + 1] if z < nz - 1 else high,
                west[z : z + 1], east[z : z + 1], no - so, wind_ref, k_ref[z],
            )
        e = jnp.swapaxes(e_ref[...], 0, 1)
        sweep(lambda i: e[i] * d_ref[i], w_ref, base_ref, nx)
        ends = (base_ref[0], base_ref[nx - 1], l_ref[0], r_ref[0], r_ref[nx - 1]) + x_faces(k_ref)
        for n, v in enumerate(ends):
            ends_ref[n] = v

    def read(ref):
        return tuple(ref[n] for n in range(5))

    def choose(test, a, b):
        return tuple(jnp.where(test, x, y) for x, y in zip(a, b))

    def ordered(own_ref, got_ref, own_first):
        own, got = read(own_ref), read(got_ref)
        return choose(own_first, own, got), choose(own_first, got, own)

    def chip_kernel(own_ref, got_ref, out_ref, near_ref, half_ref):
        b0, b1, L, C, R = merge(*ordered(own_ref, got_ref, core() == 0))
        chip = lax.axis_index("gx") // 2
        first, last = chip == 0, chip == chips - 1
        L, R = jnp.where(first, 0.0, L), jnp.where(last, 0.0, R)
        C = jnp.where(jnp.logical_or(first, last), 0.0, C)
        for n, v in enumerate((b0, b1, L, C, R)):
            out_ref[n] = near_ref[n] = v
            half_ref[n] = jnp.where(core() == 1, v[:, ny // 2 :], v[:, : ny // 2])
        near_ref[5] = own_ref[5]

    def pair_kernel(own_ref, got_ref, out_ref):
        for n, v in enumerate(merge(*ordered(own_ref, got_ref, core() == 1))):
            out_ref[n] = v

    def keep_kernel(got_ref, out_ref):
        out_ref[...] = got_ref[...]

    def side_kernel(near_ref, far_ref, half_ref, out_ref):
        for n, v in enumerate(merge(*ordered(near_ref, far_ref, core() == 1))):
            out_ref[n, :, :ny] = v
            out_ref[n, :, ny:] = half_ref[n]

    def x_finish_kernel(
        ends_ref, other_ref, side_ref, got_ref, base_ref, l_ref, r_ref, d_ref, w_ref, c_ref,
        ybase_ref, up_ref, send_ref, s_ref,
    ):
        odd = core() == 1
        chip = lax.axis_index("gx") // 2
        a, b = ordered(ends_ref, other_ref, core() == 0)
        left, right = ordered(side_ref, got_ref, core() == 0)
        opposite = tuple(jnp.concatenate([x[:, ny:], y[:, ny:]], axis=1) for x, y in zip(left, right))
        left, right = tuple(v[:, :ny] for v in left), tuple(v[:, :ny] for v in right)
        zero = jnp.zeros_like(a[0])
        lp, lg = zero, zero
        for block in (right, opposite, left):
            lp, lg = close_left(lp, lg, block)
        rp, rg = zero, zero
        for block in (left, opposite, right):
            rp, rg = close_right(rp, rg, block)
        lp, lg = jnp.where(chip == 0, 0.0, lp), jnp.where(chip == 0, 0.0, lg)
        rp, rg = jnp.where(chip == chips - 1, 0.0, rp), jnp.where(chip == chips - 1, 0.0, rg)
        ap, ag = close_left(lp, lg, a)
        bp, bg = close_right(rp, rg, b)
        last_a = (ap + ag * bp) / (1.0 - ag * bg)
        first_b = bp + bg * last_a
        first_a = (a[0] + a[2] * lp + a[3] * first_b) / (1.0 - a[2] * lg)
        last_b = (b[1] + b[4] * rp + b[3] * last_a) / (1.0 - b[4] * rg)
        before = jnp.where(odd, last_a, lp + lg * first_a)
        after = jnp.where(odd, rp + rg * last_b, first_b)
        for i in range(nx):
            s_ref[i] = base_ref[i] + l_ref[i] * before + r_ref[i] * after
        s_ref[nx], s_ref[nx + 1] = before, after
        for i in range(nx + 2, wide // nz):
            s_ref[i] = zero
        t = s_ref[...].reshape(wide, ny).T
        q = jnp.swapaxes(t.reshape(subs, steps, wide), 0, 1)
        sweep(lambda i: q[i] * d_ref[i], w_ref, ybase_ref, steps)
        b0, b1 = ybase_ref[0], ybase_ref[steps - 1]
        for level in range(3):
            shift = subs - (1 << level)
            o0, o1 = pltpu.roll(b0, shift, 0), pltpu.roll(b1, shift, 0)
            x, y, bL, aR, _, inv, _ = (c_ref[level, n] for n in range(7))
            inner = b1 + aR * o0
            up_ref[level, 0] = inner * inv
            up_ref[level, 1] = o0
            b0, b1 = b0 + x * (o0 + bL * b1), o1 + y * inner
        for n, v in enumerate((b0, b1, c_ref[3, 0], c_ref[3, 1], c_ref[3, 2])):
            send_ref[n : n + 1] = v[0:1]
        send_ref[5:8] = jnp.zeros((3, wide), jnp.float32)

    def y_finish_kernel(
        own_ref, *refs,
    ):
        got, (ybase_ref, up_ref, l_ref, r_ref, c_ref), (s_ref, t_ref, ends_ref, west, east, first_plane, second_plane) = (
            refs[: columns - 1], refs[columns - 1 : columns + 4], refs[columns + 4 :],
        )
        index = lax.axis_index("gy")
        messages = {0: own_ref[...]} | {back: ref[...] for back, ref in zip(order, got)}
        blocks = []
        for m in range(columns):
            v = messages[0]
            for back in range(1, columns):
                v = jnp.where(lax.bitwise_xor(index, back) == m, messages[back], v)
            blocks.append(tuple(v[n : n + 1] for n in range(5)))
        mine = tuple(messages[0][n : n + 1] for n in range(5))
        lp, lg, rp, rg = chain_ends(blocks, index)
        p, g = close_left(lp, lg, mine)
        last = (p + g * rp) / (1.0 - g * rg)
        right = rp + rg * last
        first = (mine[0] + mine[2] * lp + mine[3] * right) / (1.0 - mine[2] * lg)
        left = lp + lg * first
        sub = lax.broadcasted_iota(jnp.int32, (subs, wide), 0)
        L = jnp.broadcast_to(left, (subs, wide))
        R = jnp.broadcast_to(right, (subs, wide))
        for level in (2, 1, 0):
            step = 1 << level
            x, _, bL, _, bC, _, z = (c_ref[level, n] for n in range(7))
            a = up_ref[level, 0] + x * L + z * R
            b = up_ref[level, 1] + bL * a + bC * R
            upper = (sub & step) != 0
            L, R = (
                jnp.where(upper, pltpu.roll(a, step, 0), L),
                jnp.where(upper, pltpu.roll(R, step, 0), b),
            )
        ends_ref[...] = jnp.concatenate([left, right], axis=0)
        for i in range(steps):
            t_ref[i] = ybase_ref[i] + l_ref[i] * L + r_ref[i] * R
        for first in range(0, wide, 128):
            t = by_rows(t_ref, first).T
            if first < lines:
                rows = slice(first // nz, (first + 128) // nz)
                s_ref[:, rows, :] = jnp.swapaxes(t.reshape(128 // nz, nz, ny), 0, 1)
            else:
                west[...] = t[:nz]
                east[...] = t[nz : 2 * nz]
        first_plane[...], second_plane[...] = z_order(s_ref[0], s_ref[nz - 1])

    def by_rows(ref, first):
        return jnp.swapaxes(ref[:, :, first : first + 128], 0, 1).reshape(ny, 128)

    def inner_kernel(
        t_ref, ends_ref, s_ref, wind_ref, k_ref, west, east, out_ref, edge_ref, factor_ref, yd_ref, buffer, sems
    ):
        for first in range(0, lines, 128):
            s = by_rows(t_ref, first)
            left, right = (ends_ref[n : n + 1, first : first + 128] for n in range(2))
            row = lax.broadcasted_iota(jnp.int32, s.shape, 0)
            north = jnp.where(row == ny - 1, right, pltpu.roll(s, ny - 1, 0))
            south = jnp.where(row == 0, left, pltpu.roll(s, 1, 0))
            rows = slice(first // nz, (first + 128) // nz)
            yd_ref[:, rows, :] = jnp.swapaxes((north - south).T.reshape(128 // nz, nz, ny), 0, 1)
        none = jnp.zeros((nx, ny), jnp.float32)
        copies = []
        for z in range(nz):
            value = stencil(
                z, s_ref[z],
                s_ref[z - 1] if z else none,
                s_ref[z + 1] if z < nz - 1 else none,
                west[z : z + 1], east[z : z + 1], yd_ref[z], wind_ref, k_ref[z],
            )
            if 0 < z < nz - 1:
                buffer[z - 1] = value
                copies.append(pltpu.make_async_copy(buffer.at[z - 1], out_ref.at[z], sems.at[z - 1]))
                copies[-1].start()
            else:
                n = 1 if z else 0
                edge_ref[n] = value
                lift = QUARTER * wind_ref[0, z].astype(jnp.float32)
                factor_ref[n] = VERTICAL * k_ref[z] + (-lift if n else lift)
        for copy in copies:
            copy.wait()

    def final_kernel(part_ref, edge_ref, factor_ref, first, second, out_ref, buffer, sems):
        low, high = z_planes(*z_order(first[...], second[...]))
        buffer[0] = edge_ref[0] + factor_ref[0] * low
        buffer[1] = edge_ref[1] + factor_ref[1] * high
        copies = [pltpu.make_async_copy(buffer.at[n], out_ref.at[z], sems.at[n]) for n, z in enumerate((0, nz - 1))]
        for copy in copies:
            copy.start()
        for copy in copies:
            copy.wait()

    box, xbox, ybox = (nz, nx, ny), (nx, nz, ny), (steps, subs, wide)
    five = (5, nz, ny)

    def outward(a, distance):
        move = lambda i: ((i // 2 + (-distance if i % 2 else distance)) % chips) * 2 + i % 2
        return lax.ppermute(a, "gx", [(i, move(i)) for i in range(members)])

    own, give, xc = call(
        faces_kernel, [(nx + 8, ny), (nx + 8 + nz, ny), (nz, ny)], field, name="faces", flops=10**10
    )
    got = sibling(give)
    planes, edges = call(both_faces_kernel, [(2 * nx, ny), (16, lines)], own, got, name="both_faces")
    planes, edges = z_outward(planes), y_outward(edges)
    (relay,) = call(relay_kernel, [(nx + 8, ny)], planes, edges, name="relay")
    relayed = sibling(relay)
    xc = across(xc)
    dx, wx, lx, rx = call(x_matrix_kernel, [xbox] * 4, rate, name="x_matrix", flops=5 * 10**9)
    base, ends = call(
        explicit_kernel, [xbox, (7, nz, ny)],
        field, wind, rate, planes, edges, relayed, xc, got, dx, wx, lx, rx, name="explicit",
        scratch=[pltpu.VMEM(box, jnp.float32)],
    )
    other = sibling(ends)
    half = (5, nz, ny // 2)
    chip, chip_near, chip_half = call(chip_kernel, [five, (6, nz, ny), half], ends, other, name="chip")
    opposite = outward(chip_half, chips // 2)
    (opposite,) = call(keep_kernel, [half], opposite, name="keep", flops=5 * 10**9)
    near = across(chip_near)
    dy, wy, ly, ry, cy = call(
        y_matrix_kernel, [ybox] * 4 + [(4, 7, subs, wide)], dx, near, other, name="y_matrix", flops=10**6
    )
    (pair,) = call(pair_kernel, [five], chip, near, name="pair")
    distant = outward(pair, 2)
    (side,) = call(side_kernel, [(5, nz, ny + ny // 2)], near, distant, opposite, name="side")
    facing = sibling(side)
    ybase, ups, send = call(
        x_finish_kernel, [ybox, (3, 2, subs, wide), (8, wide)],
        ends, other, side, facing, base, lx, rx, dy, wy, cy, name="x_finish",
        scratch=[pltpu.VMEM((wide // nz, nz, ny), jnp.float32)],
    )
    ring = [
        lax.ppermute(send, "gy", [(i, i ^ back) for i in range(columns)])
        for back in order
    ]
    swept, turned, sides, west, east, first, second = call(
        y_finish_kernel, [box, ybox, (2, wide), (nz, ny), (nz, ny), (nx, ny), (nx, ny)],
        send, *ring, ybase, ups, ly, ry, cy, name="y_finish",
    )
    first, second = z_swap(first, 0), z_swap(second, 1)
    plane_pair = (2, nx, ny)
    part, edge, factors = call(
        inner_kernel, [box, plane_pair, plane_pair],
        turned, sides, swept, wind, rate, west, east, name="inner", flops=5 * 10**9, far_out=(0,),
        scratch=[
            pltpu.VMEM(box, jnp.float32),
            pltpu.VMEM((nz - 2, nx, ny), jnp.float32),
            pltpu.SemaphoreType.DMA((nz - 2,)),
        ],
    )
    (out,) = call(
        final_kernel, [box], part, edge, factors, first, second, name="final", far_in=(0,), far_out=(0,), alias={0: 0},
        scratch=[pltpu.VMEM(plane_pair, jnp.float32), pltpu.SemaphoreType.DMA((2,))],
    )
    return out


def solution(mesh):
    in_specs = (P("gz", "gx", "gy"), P(None, "gz", "gx", "gy"), P("gz", "gx", "gy"))
    out_specs = P("gz", "gx", "gy")
    return jax.shard_map(body, mesh=mesh, in_specs=in_specs, out_specs=out_specs, check_vma=False)
```

```python
import functools
import jax
import jax.numpy as jnp
from jax import lax
from jax.experimental import pallas as pl
from jax.experimental.pallas import tpu as pltpu
from jax.sharding import PartitionSpec as P


QUARTER = 0.25
VERTICAL = 0.06
VMEM_BYTES = 24 * 2**20


def call(kernel, outs, *ins, name, flops=0, scratch=(), far_in=(), far_out=(), alias=None):
    shapes = [jax.ShapeDtypeStruct(s, jnp.float32) for s in outs]
    vm = pl.BlockSpec(memory_space=pltpu.VMEM)
    far = pl.BlockSpec(memory_space=pl.ANY)
    size = 4 * (sum(x.size for x in ins) + sum(x.size for x in shapes))
    return pl.pallas_call(
        kernel,
        out_shape=shapes,
        in_specs=[far if n in far_in else vm for n in range(len(ins))],
        out_specs=[far if n in far_out else vm for n in range(len(outs))],
        scratch_shapes=list(scratch),
        input_output_aliases=alias or {},
        compiler_params=pltpu.CompilerParams(vmem_limit_bytes=VMEM_BYTES),
        cost_estimate=pl.CostEstimate(flops=flops, bytes_accessed=size, transcendentals=0),
        name=name,
    )(*ins)


def merge(a, b):
    a0, a1, aL, aC, aR = a
    b0, b1, bL, bC, bR = b
    inv = 1.0 / (1.0 - aR * bL)
    x = aC * inv
    y = bC * inv
    return (
        a0 + x * (b0 + bL * a1),
        b1 + y * (a1 + aR * b0),
        aL + x * bL * aC,
        x * bC,
        bR + y * aR * bC,
    )


def close_left(p, g, block):
    b0, b1, bL, bC, bR = block
    f = bC / (1.0 - bL * g)
    return b1 + bC * p + f * g * (b0 + bL * p), bR + f * g * bC


def close_right(p, g, block):
    b0, b1, bL, bC, bR = block
    f = bC / (1.0 - bR * g)
    return b0 + bC * p + f * g * (b1 + bR * p), bL + f * g * bC


def chain_ends(blocks, index):
    zero = jnp.zeros_like(blocks[0][0])
    p, g = zero, zero
    lp, lg = zero, zero
    for m in range(len(blocks) - 1):
        p, g = close_left(p, g, blocks[m])
        here = index == m + 1
        lp, lg = jnp.where(here, p, lp), jnp.where(here, g, lg)
    p, g = zero, zero
    rp, rg = zero, zero
    for m in range(len(blocks) - 1, 0, -1):
        p, g = close_right(p, g, blocks[m])
        here = index == m - 1
        rp, rg = jnp.where(here, p, rp), jnp.where(here, g, rg)
    return lp, lg, rp, rg


def factor(d_ref, w_ref, l_ref, r_ref, count):
    delta = 1.0 + d_ref[0]
    w = 1.0 / (1.0 + delta)
    w_ref[0] = w
    y = jnp.ones_like(w)
    l_ref[0] = y
    for i in range(1, count):
        y = y * w
        l_ref[i] = y
        delta = d_ref[i] + delta * w
        w = 1.0 / (1.0 + delta)
        w_ref[i] = w
    r = w
    s = w * y
    r_ref[count - 1] = r
    l_ref[count - 1] = s
    for i in range(count - 2, -1, -1):
        w = w_ref[i]
        r = w * r
        s = w * (l_ref[i] + s)
        r_ref[i] = r
        l_ref[i] = s


def sweep(q, w_ref, out_ref, count):
    y = q(0)
    out_ref[0] = y
    for i in range(1, count):
        y = q(i) + w_ref[i - 1] * y
        out_ref[i] = y
    s = w_ref[count - 1] * y
    out_ref[count - 1] = s
    for i in range(count - 2, -1, -1):
        s = w_ref[i] * (out_ref[i] + s)
        out_ref[i] = s


def stencil(z, f, below, above, west, east, ydiff, wind_ref, k):
    count = f.shape[0]
    row = lax.broadcasted_iota(jnp.int32, f.shape, 0)
    e = jnp.where(row == count - 1, east, pltpu.roll(f, count - 1, 0))
    w = jnp.where(row == 0, west, pltpu.roll(f, 1, 0))
    wz = wind_ref[0, z].astype(jnp.float32)
    wx = wind_ref[1, z].astype(jnp.float32)
    wy = wind_ref[2, z].astype(jnp.float32)
    return (
        f
        - QUARTER * (wz * (above - below) + wx * (e - w) + wy * ydiff)
        + VERTICAL * k * (above + below - 2.0 * f)
    )


def body(field, wind, rate):
    nz, nx, ny = field.shape
    lines = nz * nx
    members = lax.axis_size("gx")
    chips = members // 2
    levels = lax.axis_size("gz")
    columns = lax.axis_size("gy")
    reach = nx * members / 8.0
    c = reach * reach
    subs = 8
    steps = ny // subs
    wide = -(-(lines + 2 * nz) // 128) * 128
    order = (1, 3, 2)

    def core():
        return lax.rem(lax.axis_index("gx"), 2)

    def faces_kernel(f_ref, own, give, xc):
        odd = core() == 1
        low, high = f_ref[0], f_ref[nz - 1]
        own[0:nx] = jnp.where(odd, high, low)
        give[0:nx] = jnp.where(odd, low, high)
        flat = f_ref[...].reshape(lines, ny)
        low = flat[:, :128].T[:1]
        high = flat[:, ny - 128 :].T[127:]
        pad = jnp.zeros((7, lines), jnp.float32)
        own[nx : nx + 8] = jnp.concatenate([jnp.where(odd, high, low), pad], axis=0)
        give[nx : nx + 8] = jnp.concatenate([jnp.where(odd, low, high), pad], axis=0)
        xc[0:nz], give[nx + 8 :] = x_faces(f_ref)

    def x_faces(ref):
        odd = core() == 1
        first, last = ref[:, 0, :], ref[:, nx - 1, :]
        return jnp.where(odd, last, first), jnp.where(odd, first, last)

    def both_faces_kernel(own, got, planes, columns_out):
        planes[0:nx] = got[0:nx]
        planes[nx:] = own[0:nx]
        columns_out[0:8] = got[nx : nx + 8]
        columns_out[8:16] = own[nx:]

    def relay_kernel(planes, columns_in, out_ref):
        out_ref[0:nx] = planes[nx:]
        out_ref[nx:] = columns_in[8:16]

    def y_outward(a):
        pairs = []
        for x in range(members):
            for y in range(columns):
                pairs.append((x * columns + y, (x ^ 1) * columns + (y + (1 if x % 2 else -1)) % columns))
        return lax.ppermute(a, ("gx", "gy"), pairs)

    def z_outward(a):
        pairs = []
        for z in range(levels):
            for x in range(members):
                to = z + (1 if x % 2 else -1)
                pairs.append((z * members + x, to * members + (x ^ 1) if 0 <= to < levels else z * members + (x ^ 2)))
        return lax.ppermute(a, ("gz", "gx"), pairs)

    def z_swap(a, parity):
        pairs = []
        for z in range(levels):
            for x in range(members):
                to = z + (1 if (z + x) % 2 == parity else -1)
                pairs.append((z * members + x, to * members + x if 0 <= to < levels else z * members + (x ^ 2)))
        return lax.ppermute(a, ("gz", "gx"), pairs)

    def z_order(low, high):
        even = lax.rem(lax.axis_index("gz") + lax.axis_index("gx"), 2) == 0
        return jnp.where(even, high, low), jnp.where(even, low, high)

    def across(a):
        return lax.ppermute(a, "gx", [(i, (i + 1 if i % 2 else i - 1) % members) for i in range(members)])

    def sibling(a):
        return lax.ppermute(a, "gx", [(i, i ^ 1) for i in range(members)])

    def x_sides(cross, inner):
        odd = core() == 1
        return jnp.where(odd, inner, cross), jnp.where(odd, cross, inner)

    def x_rows(cross, inner):
        index = lax.axis_index("gx")
        west, east = x_sides(cross, inner)
        return jnp.where(index == 0, 0.0, west), jnp.where(index == members - 1, 0.0, east)

    def z_planes(below, above):
        index = lax.axis_index("gz")
        return jnp.where(index == 0, 0.0, below), jnp.where(index == levels - 1, 0.0, above)

    def x_matrix_kernel(k_ref, d_ref, w_ref, l_ref, r_ref):
        d_ref[...] = 1.0 / (c * jnp.swapaxes(k_ref[...], 0, 1))
        factor(d_ref, w_ref, l_ref, r_ref, nx)

    def y_matrix_kernel(x_ref, near_ref, other_ref, d_ref, w_ref, l_ref, r_ref, c_ref):
        west, east = x_sides(near_ref[5], other_ref[6])
        d = jnp.concatenate(
            [
                x_ref[...].reshape(lines, ny),
                1.0 / (c * west),
                1.0 / (c * east),
                jnp.ones((wide - lines - 2 * nz, ny), jnp.float32),
            ],
            axis=0,
        )
        d_ref[...] = jnp.swapaxes(d.T.reshape(subs, steps, wide), 0, 1)
        factor(d_ref, w_ref, l_ref, r_ref, steps)
        L, C, R = l_ref[0], r_ref[0], r_ref[steps - 1]
        for level in range(3):
            shift = subs - (1 << level)
            bL, bC, bR = pltpu.roll(L, shift, 0), pltpu.roll(C, shift, 0), pltpu.roll(R, shift, 0)
            inv = 1.0 / (1.0 - R * bL)
            x, y = C * inv, bC * inv
            for n, value in enumerate((x, y, bL, R, bC, inv, R * y)):
                c_ref[level, n] = value
            L, C, R = L + x * bL * C, x * bC, bR + y * R * bC
        for n, value in enumerate((L, C, R)):
            c_ref[3, n] = value
        for n in range(3, 7):
            c_ref[3, n] = jnp.zeros_like(L)

    def explicit_kernel(
        f_ref, wind_ref, k_ref, planes, columns_in, relayed, xc, got, d_ref, w_ref, l_ref, r_ref,
        base_ref, ends_ref, e_ref,
    ):
        west, east = x_rows(xc[0:nz], got[nx + 8 :])
        odd = core() == 1
        low, high = z_planes(*choose(odd, (relayed[0:nx], planes[0:nx]), (planes[0:nx], relayed[0:nx])))
        gy = lax.axis_index("gy")
        near, far = columns_in[0:1], relayed[nx : nx + 1]
        left = jnp.where(gy == 0, 0.0, jnp.where(odd, far, near))
        right = jnp.where(gy == columns - 1, 0.0, jnp.where(odd, near, far))
        left = jnp.broadcast_to(left, (128, lines)).T
        right = jnp.broadcast_to(right, (128, lines)).T
        lane = lax.broadcasted_iota(jnp.int32, (nx, 128), 1)
        for z in range(nz):
            f = f_ref[z]
            rows = slice(z * nx, (z + 1) * nx)
            no = pltpu.roll(f, ny - 1, 1)
            so = pltpu.roll(f, 1, 1)
            no = jnp.concatenate([no[:, : ny - 128], jnp.where(lane == 127, right[rows], no[:, ny - 128 :])], axis=1)
            so = jnp.concatenate([jnp.where(lane == 0, left[rows], so[:, :128]), so[:, 128:]], axis=1)
            e_ref[z] = stencil(
                z, f,
                f_ref[z - 1] if z else low,
                f_ref[z + 1] if z < nz - 1 else high,
                west[z : z + 1], east[z : z + 1], no - so, wind_ref, k_ref[z],
            )
        e = jnp.swapaxes(e_ref[...], 0, 1)
        sweep(lambda i: e[i] * d_ref[i], w_ref, base_ref, nx)
        ends = (base_ref[0], base_ref[nx - 1], l_ref[0], r_ref[0], r_ref[nx - 1]) + x_faces(k_ref)
        for n, v in enumerate(ends):
            ends_ref[n] = v

    def read(ref):
        return tuple(ref[n] for n in range(5))

    def choose(test, a, b):
        return tuple(jnp.where(test, x, y) for x, y in zip(a, b))

    def ordered(own_ref, got_ref, own_first):
        own, got = read(own_ref), read(got_ref)
        return choose(own_first, own, got), choose(own_first, got, own)

    def chip_kernel(own_ref, got_ref, out_ref, near_ref, half_ref):
        b0, b1, L, C, R = merge(*ordered(own_ref, got_ref, core() == 0))
        chip = lax.axis_index("gx") // 2
        first, last = chip == 0, chip == chips - 1
        L, R = jnp.where(first, 0.0, L), jnp.where(last, 0.0, R)
        C = jnp.where(jnp.logical_or(first, last), 0.0, C)
        for n, v in enumerate((b0, b1, L, C, R)):
            out_ref[n] = near_ref[n] = v
            half_ref[n] = jnp.where(core() == 1, v[:, ny // 2 :], v[:, : ny // 2])
        near_ref[5] = own_ref[5]

    def pair_kernel(own_ref, got_ref, out_ref):
        for n, v in enumerate(merge(*ordered(own_ref, got_ref, core() == 1))):
            out_ref[n] = v

    def keep_kernel(got_ref, out_ref):
        out_ref[...] = got_ref[...]

    def side_kernel(near_ref, far_ref, half_ref, out_ref):
        for n, v in enumerate(merge(*ordered(near_ref, far_ref, core() == 1))):
            out_ref[n, :, :ny] = v
            out_ref[n, :, ny:] = half_ref[n]

    def x_finish_kernel(
        ends_ref, other_ref, side_ref, got_ref, base_ref, l_ref, r_ref, d_ref, w_ref, c_ref,
        ybase_ref, up_ref, send_ref, s_ref,
    ):
        odd = core() == 1
        chip = lax.axis_index("gx") // 2
        a, b = ordered(ends_ref, other_ref, core() == 0)
        left, right = ordered(side_ref, got_ref, core() == 0)
        opposite = tuple(jnp.concatenate([x[:, ny:], y[:, ny:]], axis=1) for x, y in zip(left, right))
        left, right = tuple(v[:, :ny] for v in left), tuple(v[:, :ny] for v in right)
        zero = jnp.zeros_like(a[0])
        lp, lg = zero, zero
        for block in (right, opposite, left):
            lp, lg = close_left(lp, lg, block)
        rp, rg = zero, zero
        for block in (left, opposite, right):
            rp, rg = close_right(rp, rg, block)
        lp, lg = jnp.where(chip == 0, 0.0, lp), jnp.where(chip == 0, 0.0, lg)
        rp, rg = jnp.where(chip == chips - 1, 0.0, rp), jnp.where(chip == chips - 1, 0.0, rg)
        ap, ag = close_left(lp, lg, a)
        bp, bg = close_right(rp, rg, b)
        last_a = (ap + ag * bp) / (1.0 - ag * bg)
        first_b = bp + bg * last_a
        first_a = (a[0] + a[2] * lp + a[3] * first_b) / (1.0 - a[2] * lg)
        last_b = (b[1] + b[4] * rp + b[3] * last_a) / (1.0 - b[4] * rg)
        before = jnp.where(odd, last_a, lp + lg * first_a)
        after = jnp.where(odd, rp + rg * last_b, first_b)
        for i in range(nx):
            s_ref[i] = base_ref[i] + l_ref[i] * before + r_ref[i] * after
        s_ref[nx], s_ref[nx + 1] = before, after
        for i in range(nx + 2, wide // nz):
            s_ref[i] = zero
        t = s_ref[...].reshape(wide, ny).T
        q = jnp.swapaxes(t.reshape(subs, steps, wide), 0, 1)
        sweep(lambda i: q[i] * d_ref[i], w_ref, ybase_ref, steps)
        b0, b1 = ybase_ref[0], ybase_ref[steps - 1]
        for level in range(3):
            shift = subs - (1 << level)
            o0, o1 = pltpu.roll(b0, shift, 0), pltpu.roll(b1, shift, 0)
            x, y, bL, aR, _, inv, _ = (c_ref[level, n] for n in range(7))
            inner = b1 + aR * o0
            up_ref[level, 0] = inner * inv
            up_ref[level, 1] = o0
            b0, b1 = b0 + x * (o0 + bL * b1), o1 + y * inner
        for n, v in enumerate((b0, b1, c_ref[3, 0], c_ref[3, 1], c_ref[3, 2])):
            send_ref[n : n + 1] = v[0:1]
        send_ref[5:8] = jnp.zeros((3, wide), jnp.float32)

    def y_finish_kernel(
        own_ref, *refs,
    ):
        got, (ybase_ref, up_ref, l_ref, r_ref, c_ref), (s_ref, t_ref, ends_ref, west, east, first_plane, second_plane) = (
            refs[: columns - 1], refs[columns - 1 : columns + 4], refs[columns + 4 :],
        )
        index = lax.axis_index("gy")
        messages = {0: own_ref[...]} | {back: ref[...] for back, ref in zip(order, got)}
        blocks = []
        for m in range(columns):
            v = messages[0]
            for back in range(1, columns):
                v = jnp.where(lax.bitwise_xor(index, back) == m, messages[back], v)
            blocks.append(tuple(v[n : n + 1] for n in range(5)))
        mine = tuple(messages[0][n : n + 1] for n in range(5))
        lp, lg, rp, rg = chain_ends(blocks, index)
        p, g = close_left(lp, lg, mine)
        last = (p + g * rp) / (1.0 - g * rg)
        right = rp + rg * last
        first = (mine[0] + mine[2] * lp + mine[3] * right) / (1.0 - mine[2] * lg)
        left = lp + lg * first
        sub = lax.broadcasted_iota(jnp.int32, (subs, wide), 0)
        L = jnp.broadcast_to(left, (subs, wide))
        R = jnp.broadcast_to(right, (subs, wide))
        for level in (2, 1, 0):
            step = 1 << level
            x, _, bL, _, bC, _, z = (c_ref[level, n] for n in range(7))
            a = up_ref[level, 0] + x * L + z * R
            b = up_ref[level, 1] + bL * a + bC * R
            upper = (sub & step) != 0
            L, R = (
                jnp.where(upper, pltpu.roll(a, step, 0), L),
                jnp.where(upper, pltpu.roll(R, step, 0), b),
            )
        ends_ref[...] = jnp.concatenate([left, right], axis=0)
        for i in range(steps):
            t_ref[i] = ybase_ref[i] + l_ref[i] * L + r_ref[i] * R
        for first in range(0, wide, 128):
            t = by_rows(t_ref, first).T
            if first < lines:
                rows = slice(first // nz, (first + 128) // nz)
                s_ref[:, rows, :] = jnp.swapaxes(t.reshape(128 // nz, nz, ny), 0, 1)
            else:
                west[...] = t[:nz]
                east[...] = t[nz : 2 * nz]
        first_plane[...], second_plane[...] = z_order(s_ref[0], s_ref[nz - 1])

    def by_rows(ref, first):
        return jnp.swapaxes(ref[:, :, first : first + 128], 0, 1).reshape(ny, 128)

    def inner_kernel(
        t_ref, ends_ref, s_ref, wind_ref, k_ref, west, east, out_ref, edge_ref, factor_ref, yd_ref, buffer, sems
    ):
        for first in range(0, lines, 128):
            s = by_rows(t_ref, first)
            left, right = (ends_ref[n : n + 1, first : first + 128] for n in range(2))
            row = lax.broadcasted_iota(jnp.int32, s.shape, 0)
            north = jnp.where(row == ny - 1, right, pltpu.roll(s, ny - 1, 0))
            south = jnp.where(row == 0, left, pltpu.roll(s, 1, 0))
            rows = slice(first // nz, (first + 128) // nz)
            yd_ref[:, rows, :] = jnp.swapaxes((north - south).T.reshape(128 // nz, nz, ny), 0, 1)
        none = jnp.zeros((nx, ny), jnp.float32)
        copies = []
        for z in range(nz):
            value = stencil(
                z, s_ref[z],
                s_ref[z - 1] if z else none,
                s_ref[z + 1] if z < nz - 1 else none,
                west[z : z + 1], east[z : z + 1], yd_ref[z], wind_ref, k_ref[z],
            )
            if 0 < z < nz - 1:
                buffer[z - 1] = value
                copies.append(pltpu.make_async_copy(buffer.at[z - 1], out_ref.at[z], sems.at[z - 1]))
                copies[-1].start()
            else:
                n = 1 if z else 0
                edge_ref[n] = value
                lift = QUARTER * wind_ref[0, z].astype(jnp.float32)
                factor_ref[n] = VERTICAL * k_ref[z] + (-lift if n else lift)
        for copy in copies:
            copy.wait()

    def final_kernel(part_ref, edge_ref, factor_ref, first, second, out_ref, buffer, sems):
        low, high = z_planes(*z_order(first[...], second[...]))
        buffer[0] = edge_ref[0] + factor_ref[0] * low
        buffer[1] = edge_ref[1] + factor_ref[1] * high
        copies = [pltpu.make_async_copy(buffer.at[n], out_ref.at[z], sems.at[n]) for n, z in enumerate((0, nz - 1))]
        for copy in copies:
            copy.start()
        for copy in copies:
            copy.wait()

    box, xbox, ybox = (nz, nx, ny), (nx, nz, ny), (steps, subs, wide)
    five = (5, nz, ny)

    def outward(a, distance):
        move = lambda i: ((i // 2 + (-distance if i % 2 else distance)) % chips) * 2 + i % 2
        return lax.ppermute(a, "gx", [(i, move(i)) for i in range(members)])

    own, give, xc = call(
        faces_kernel, [(nx + 8, ny), (nx + 8 + nz, ny), (nz, ny)], field, name="faces", flops=10**10
    )
    got = sibling(give)
    planes, edges = call(both_faces_kernel, [(2 * nx, ny), (16, lines)], own, got, name="both_faces")
    planes, edges = z_outward(planes), y_outward(edges)
    (relay,) = call(relay_kernel, [(nx + 8, ny)], planes, edges, name="relay")
    relayed = sibling(relay)
    xc = across(xc)
    dx, wx, lx, rx = call(x_matrix_kernel, [xbox] * 4, rate, name="x_matrix", flops=5 * 10**9)
    base, ends = call(
        explicit_kernel, [xbox, (7, nz, ny)],
        field, wind, rate, planes, edges, relayed, xc, got, dx, wx, lx, rx, name="explicit",
        scratch=[pltpu.VMEM(box, jnp.float32)],
    )
    other = sibling(ends)
    half = (5, nz, ny // 2)
    chip, chip_near, chip_half = call(chip_kernel, [five, (6, nz, ny), half], ends, other, name="chip")
    opposite = outward(chip_half, chips // 2)
    (opposite,) = call(keep_kernel, [half], opposite, name="keep", flops=5 * 10**9)
    near = across(chip_near)
    dy, wy, ly, ry, cy = call(
        y_matrix_kernel, [ybox] * 4 + [(4, 7, subs, wide)], dx, near, other, name="y_matrix", flops=10**6
    )
    (pair,) = call(pair_kernel, [five], chip, near, name="pair")
    distant = outward(pair, 2)
    (side,) = call(side_kernel, [(5, nz, ny + ny // 2)], near, distant, opposite, name="side")
    facing = sibling(side)
    ybase, ups, send = call(
        x_finish_kernel, [ybox, (3, 2, subs, wide), (8, wide)],
        ends, other, side, facing, base, lx, rx, dy, wy, cy, name="x_finish",
        scratch=[pltpu.VMEM((wide // nz, nz, ny), jnp.float32)],
    )
    ring = [
        lax.ppermute(send, "gy", [(i, i ^ back) for i in range(columns)])
        for back in order
    ]
    swept, turned, sides, west, east, first, second = call(
        y_finish_kernel, [box, ybox, (2, wide), (nz, ny), (nz, ny), (nx, ny), (nx, ny)],
        send, *ring, ybase, ups, ly, ry, cy, name="y_finish",
    )
    first, second = z_swap(first, 0), z_swap(second, 1)
    plane_pair = (2, nx, ny)
    part, edge, factors = call(
        inner_kernel, [box, plane_pair, plane_pair],
        turned, sides, swept, wind, rate, west, east, name="inner", flops=5 * 10**9, far_out=(0,),
        scratch=[
            pltpu.VMEM(box, jnp.float32),
            pltpu.VMEM((nz - 2, nx, ny), jnp.float32),
            pltpu.SemaphoreType.DMA((nz - 2,)),
        ],
    )
    (out,) = call(
        final_kernel, [box], part, edge, factors, first, second, name="final", far_in=(0,), far_out=(0,), alias={0: 0},
        scratch=[pltpu.VMEM(plane_pair, jnp.float32), pltpu.SemaphoreType.DMA((2,))],
    )
    return out


def solution(mesh):
    in_specs = (P("gz", "gx", "gy"), P(None, "gz", "gx", "gy"), P("gz", "gx", "gy"))
    out_specs = P("gz", "gx", "gy")
    return jax.shard_map(body, mesh=mesh, in_specs=in_specs, out_specs=out_specs, check_vma=False)
```
